512 devices in a mesh: head: 2 (over y_hi), outer: 8 (over x, core), inner: 32 (over y_lo, z).
Axes of the slice: x: 4, y: 4 (y_hi: 2, y_lo: 2; y = y_hi * 2 + y_lo), z: 16, core: 2. Of those that a mesh axis runs over, the one named last changes fastest.
Arguments:
- query: bfloat16 [32768, 32, 128], P(('outer', 'inner'), 'head'), may hold values from -100 to 100
- grad_out: bfloat16 [32768, 32, 128], P(('outer', 'inner'), 'head'), may hold values from -60 to 60
- out_forward: bfloat16 [32768, 32, 128], P(('outer', 'inner'), 'head'), may hold values from -4 to 4
- k_codes: int32 [32768, 4, 128], P(('outer', 'inner'), 'head'), may hold values from 0 to 15
- k_scale: float32 [4, 128], P('head'), may hold values from 0.15 to 0.45
- k_offset: float32 [4, 128], P('head'), may hold values from 0.975 to 3.825, as said below
- v_codes: int32 [32768, 4, 128], P(('outer', 'inner'), 'head'), may hold values from 0 to 15
- v_scale: float32 [4, 128], P('head'), may hold values from 0.15 to 0.45
- v_offset: float32 [4, 128], P('head'), may hold values from 1.5 to 2.5
Outputs:
- query_grad: bfloat16 [32768, 32, 128], P(('outer', 'inner'), 'head')
- key_grad: bfloat16 [32768, 4, 128], P(('outer', 'inner'), 'head')
- value_grad: bfloat16 [32768, 4, 128], P(('outer', 'inner'), 'head')
- quant_grads: float32 [4, 4, 128], P(None, 'head')
The draws below stay inside these ranges and needn't reach their ends.
Inputs may be any that keep to these rules, and one draw needn't show every extreme that they name: `k_offset`: each channel's offset lies between 6.5 and 8.5 times its step.
All inputs are finite; a program needn't handle non-finite values.
Results may differ from the reference program's by a relative error of at most 0.04.
Values may be sent and summed in bfloat16 or wider, within the bound.
No kernel may reach another device: no remote copies, remote signals or barrier semaphores. Data moves between devices by JAX's collectives and lax.ppermute only.
A program may use at most 64 MiB of HBM per device.

```python
import math
import jax
import jax.numpy as jnp
from jax import lax

HD = 128
KVHEADS = 4
GROUP = 8
QHEADS = 32
TOK_DEV = 128
TOKENS = 32768
WIN = 512


def key_parts(key):
    codes = jax.random.randint(jax.random.fold_in(key, 101), (TOKENS, KVHEADS, HD), 0, 16, dtype=jnp.int32)
    scales = jnp.exp(jax.random.uniform(jax.random.fold_in(key, 102), (KVHEADS, HD), jnp.float32, math.log(0.15), math.log(0.45)))
    offsets = scales * jax.random.uniform(jax.random.fold_in(key, 103), (KVHEADS, HD), jnp.float32, 6.5, 8.5)
    return (codes, scales, offsets)


def draw_k_codes(key, part):
    shared = key_parts(key)
    return shared[0]


def draw_k_scale(key, part):
    shared = key_parts(key)
    return shared[1]


def draw_k_offset(key, part):
    shared = key_parts(key)
    return shared[2]


def draw_query(key, part):
    key = jax.random.fold_in(key, 4)
    base = jax.random.truncated_normal(key, -6.0, 6.0, (TOKENS, QHEADS, HD), jnp.float32)
    return base.astype(jnp.bfloat16)


def draw_grad_out(key, part):
    key = jax.random.fold_in(key, 5)
    positions = jnp.arange(TOKENS, dtype=jnp.float32)
    heads = jnp.arange(QHEADS, dtype=jnp.float32)
    spread = (1.0 + 2.0 * positions / (TOKENS - 1))[:, None, None] * (3.0 ** (heads / QHEADS))[None, :, None]
    values = spread * jax.random.truncated_normal(key, -6.0, 6.0, (TOKENS, QHEADS, HD), jnp.float32)
    return values.astype(jnp.bfloat16)


def place_ends(array, stream_key, least, largest):
    index_at = [jax.random.randint(jax.random.fold_in(stream_key, axis), (), 0, length) for axis, length in enumerate(array.shape)]
    longest = array.shape.index(max(array.shape))
    neighbour = index_at[:longest] + [(index_at[longest] + 1) % array.shape[longest]] + index_at[longest + 1:]
    return array.at[tuple(index_at)].set(least).at[tuple(neighbour)].set(largest)


def block_levels(stream_key, shape, shards, least, high):
    gain = 1.0
    for position, shards_of in shards:
        steps = jax.random.uniform(jax.random.fold_in(jax.random.fold_in(stream_key, 6), position), (shards_of,), jnp.float32, least / len(shards), high / len(shards))
        gain = gain * jnp.repeat(jnp.exp(steps), shape[position] // shards_of).reshape((-1,) + (1,) * (len(shape) - 1 - position))
    return gain


def scatter_about(own_key, extent, scale, limit, pieces=(), held_as=jnp.bfloat16):
    drawn = jax.random.normal(own_key, extent, jnp.float32) * scale
    if len(pieces) > 0:
        drawn = block_levels(own_key, extent, pieces, -0.22, 0.18) * drawn
    return jnp.clip(drawn, min=-limit, max=limit).astype(held_as)


def setup_inputs(seed: int = 0) -> dict:
    key_of = jax.random.split(jax.random.key(seed), 10)
    return {
        "query": draw_query(jax.random.fold_in(key_of[9], 71), 0),
        "grad_out": draw_grad_out(jax.random.fold_in(key_of[9], 71), 0),
        "out_forward": scatter_about(key_of[2], (TOKENS, QHEADS, HD), 0.3, 4.0, ((0, 256), (1, 2))),
        "k_codes": draw_k_codes(jax.random.fold_in(key_of[9], 71), 0),
        "k_scale": draw_k_scale(jax.random.fold_in(key_of[9], 71), 0),
        "k_offset": draw_k_offset(jax.random.fold_in(key_of[9], 71), 0),
        "v_codes": place_ends(jax.random.randint(key_of[6], (TOKENS, KVHEADS, HD), 0, 16), jax.random.fold_in(key_of[6], 1), 0, 15).astype(jnp.int32),
        "v_scale": jnp.clip(jnp.exp(math.log(0.45) - 1.0986122 * jax.random.uniform(key_of[7], (KVHEADS, HD), jnp.float32) ** block_levels(key_of[7], (KVHEADS, HD), ((0, 2),), -0.2, 0.2)), 0.15, 0.45),
        "v_offset": jnp.clip(1.5 + 1.0 * jax.random.uniform(key_of[8], (KVHEADS, HD), jnp.float32) ** block_levels(key_of[8], (KVHEADS, HD), ((0, 2),), -0.2, 0.2), 1.5, 2.5),
    }


clip_limit = 16.0
rope_base = 500000.0

def rope_tables(positions):
    freqs = rope_base ** (-jnp.arange(0, HD, 2, dtype=jnp.float32) / HD)
    angles = positions.astype(jnp.float32)[:, None] * freqs[None, :]
    angles = jnp.concatenate([angles, angles], axis=-1)
    return (jnp.cos(angles)[:, None, :], jnp.sin(angles)[:, None, :])

def rotate(values, cosines, sines):
    half = values.shape[-1] // 2
    turned = jnp.concatenate([-values[..., half:], values[..., :half]], axis=-1)
    return values * cosines + turned * sines

def rotate_back(grads, cosines, sines):
    half = grads.shape[-1] // 2
    scaled = grads * sines
    turned = jnp.concatenate([scaled[..., half:], -scaled[..., :half]], axis=-1)
    return grads * cosines + turned

def hadamard_table(order):
    index = jnp.arange(order, dtype=jnp.int32)
    common = jnp.bitwise_and(index[:, None], index[None, :])
    parity = jnp.zeros((order, order), jnp.int32)
    for level in range(order.bit_length() - 1):
        parity = parity + jnp.bitwise_and(jnp.right_shift(common, level), 1)
    signs = 1 - 2 * (parity % 2)
    return signs.astype(jnp.float32) / math.sqrt(order)

def reference(query, grad_out, out_forward, k_codes, k_scale, k_offset, v_codes, v_scale, v_offset):
    scale = 1.0 / math.sqrt(HD)
    positions = jnp.arange(TOKENS, dtype=jnp.int32)
    cosines, sines = rope_tables(positions)
    key_codes = k_codes.astype(jnp.float32)
    value_codes = v_codes.astype(jnp.float32)
    key_deq = k_scale[None] * key_codes - k_offset[None]
    key_fq = rotate(key_deq, cosines, sines).astype(jnp.bfloat16)
    hadamard = hadamard_table(HD)
    value_deq = v_scale[None] * value_codes - v_offset[None]
    value_fq = jnp.einsum('tkd,de->tke', value_deq, hadamard, precision=lax.Precision.HIGHEST).astype(jnp.bfloat16)
    delta = lax.optimization_barrier(jnp.sum(grad_out.astype(jnp.float32) * out_forward.astype(jnp.float32), axis=-1))
    padding = jnp.zeros((WIN, KVHEADS, HD), jnp.bfloat16)
    key_pad = jnp.concatenate([padding, key_fq], axis=0)
    value_pad = jnp.concatenate([padding, value_fq], axis=0)
    span = WIN + TOK_DEV
    row_index = jnp.arange(TOK_DEV, dtype=jnp.int32)[:, None]
    col_index = jnp.arange(span, dtype=jnp.int32)[None, :]

    def block_step(carry, index):
        key_acc, value_acc = carry
        start = (index * TOK_DEV).astype(jnp.int32)
        queries = lax.dynamic_slice_in_dim(query, start, TOK_DEV, 0).astype(jnp.float32).reshape(TOK_DEV, KVHEADS, GROUP, HD)
        upstream_rows = lax.dynamic_slice_in_dim(grad_out, start, TOK_DEV, 0).astype(jnp.float32).reshape(TOK_DEV, KVHEADS, GROUP, HD)
        block_delta = jnp.transpose(lax.dynamic_slice_in_dim(delta, start, TOK_DEV, 0).reshape(TOK_DEV, KVHEADS, GROUP), (1, 2, 0))
        keys = lax.dynamic_slice_in_dim(key_pad, start, span, 0).astype(jnp.float32)
        values = lax.dynamic_slice_in_dim(value_pad, start, span, 0).astype(jnp.float32)
        gap = row_index + WIN - col_index
        valid = (gap >= 0) & (gap < WIN) & (col_index + start >= WIN)
        scores = jnp.einsum('tkgd,ukd->kgtu', queries, keys) * scale
        top = lax.optimization_barrier(jnp.max(jnp.where(valid, scores, -jnp.inf), axis=-1, keepdims=True))
        total = lax.optimization_barrier(jnp.sum(jnp.where(valid, jnp.exp(scores - top), 0.0), axis=-1, keepdims=True))
        weights = jnp.where(valid, jnp.exp(scores - (top + jnp.log(total))), 0.0)
        weights_low = lax.optimization_barrier(weights.astype(jnp.bfloat16)).astype(jnp.float32)
        upstream = jnp.einsum('tkgd,ukd->kgtu', upstream_rows, values)
        score_grad = weights * (upstream - block_delta[..., None])
        score_grad = lax.optimization_barrier(score_grad.astype(jnp.bfloat16)).astype(jnp.float32)
        query_block = (jnp.einsum('kgtu,ukd->tkgd', score_grad, keys) * scale).reshape(TOK_DEV, QHEADS, HD).astype(jnp.bfloat16)
        key_part = jnp.einsum('kgtu,tkgd->ukd', score_grad, queries) * scale
        value_part = jnp.einsum('kgtu,tkgd->ukd', weights_low, upstream_rows)
        key_acc = lax.dynamic_update_slice_in_dim(key_acc, lax.dynamic_slice_in_dim(key_acc, start, span, 0) + key_part, start, 0)
        value_acc = lax.dynamic_update_slice_in_dim(value_acc, lax.dynamic_slice_in_dim(value_acc, start, span, 0) + value_part, start, 0)
        return ((key_acc, value_acc), query_block)
    zeros = jnp.zeros((WIN + TOKENS, KVHEADS, HD), jnp.float32)
    (key_acc, value_acc), query_blocks = lax.scan(block_step, (zeros, zeros), jnp.arange(TOKENS // TOK_DEV, dtype=jnp.int32))
    query_grad = query_blocks.reshape(TOKENS, QHEADS, HD)
    key_deq_grad = rotate_back(key_acc[WIN:], cosines, sines)
    value_deq_grad = jnp.einsum('tke,de->tkd', value_acc[WIN:], hadamard, precision=lax.Precision.HIGHEST)
    key_grad = jnp.where((k_codes > 0) & (k_codes < 15), key_deq_grad, 0.0).astype(jnp.bfloat16)
    value_grad = jnp.where((v_codes > 0) & (v_codes < 15), value_deq_grad, 0.0).astype(jnp.bfloat16)
    raw = jnp.stack([lax.optimization_barrier(jnp.sum(key_deq_grad * key_codes, axis=0)), -lax.optimization_barrier(jnp.sum(key_deq_grad, axis=0)), lax.optimization_barrier(jnp.sum(value_deq_grad * value_codes, axis=0)), -lax.optimization_barrier(jnp.sum(value_deq_grad, axis=0))])
    factor = jnp.minimum(1.0, clip_limit / jnp.sqrt(jnp.sum(raw * raw) + 1e-06))
    return (query_grad, key_grad, value_grad, raw * factor)
```

```python
import math

import jax
import jax.numpy as jnp
from jax import lax
from jax.sharding import Mesh, PartitionSpec as P

WIN = 512
clip_limit = 16.0
rope_base = 500000.0
TOK = ("x", "core", "ylo", "z")
FLAT = ("head", "x", "core", "ylo")


def shift(value, by):
    count = 1
    for axis in TOK:
        count *= lax.axis_size(axis)
    pairs = [(i, i + by) for i in range(count) if 0 <= i + by < count]
    return lax.ppermute(value, TOK, pairs)


def gather_all(value, axes):
    count = 1
    for axis in (axes,) if isinstance(axes, str) else axes:
        count *= lax.axis_size(axis)
    spread = jnp.broadcast_to(value[None], (count,) + value.shape)
    return lax.all_to_all(spread, axes, 0, 0)


def rope_tables(positions, head_size):
    freqs = rope_base ** (-jnp.arange(0, head_size, 2, dtype=jnp.float32) / head_size)
    angles = positions.astype(jnp.float32)[:, None] * freqs[None, :]
    angles = jnp.concatenate([angles, angles], axis=-1)
    return (jnp.cos(angles)[:, None, :], jnp.sin(angles)[:, None, :])


def rotate(values, cosines, sines):
    half = values.shape[-1] // 2
    turned = jnp.concatenate([-values[..., half:], values[..., :half]], axis=-1)
    return values * cosines + turned * sines


def rotate_back(grads, cosines, sines):
    half = grads.shape[-1] // 2
    scaled = grads * sines
    turned = jnp.concatenate([scaled[..., half:], -scaled[..., :half]], axis=-1)
    return grads * cosines + turned


def hadamard_table(order):
    index = jnp.arange(order, dtype=jnp.int32)
    common = jnp.bitwise_and(index[:, None], index[None, :])
    parity = jnp.zeros((order, order), jnp.int32)
    for level in range(order.bit_length() - 1):
        parity = parity + jnp.bitwise_and(jnp.right_shift(common, level), 1)
    signs = 1 - 2 * (parity % 2)
    return signs.astype(jnp.float32) / math.sqrt(order)


def body(query, grad_out, out_forward, k_codes, k_scale, k_offset, v_codes, v_scale, v_offset):
    block_rows, query_heads, head_size = query.shape
    kv_heads = k_codes.shape[1]
    group = query_heads // kv_heads
    reach = WIN // block_rows
    scale = 1.0 / math.sqrt(head_size)
    device_block = jnp.int32(0)
    for axis in TOK:
        device_block = device_block * lax.axis_size(axis) + lax.axis_index(axis)
    hadamard = hadamard_table(head_size)

    own = jnp.stack([k_codes, v_codes]).astype(jnp.bfloat16)
    one = shift(own, 1)
    two = shift(own, 2)
    far = shift(jnp.stack([one, two]), 2)
    codes = [own, one, two, far[0], far[1]]

    tables = []
    for distance in range(reach + 1):
        first_row = (device_block - distance) * block_rows
        tables.append(rope_tables(first_row + jnp.arange(block_rows, dtype=jnp.int32), head_size))

    def key_block(distance):
        deq = k_scale[None] * codes[distance][0].astype(jnp.float32) - k_offset[None]
        return rotate(deq, *tables[distance]).astype(jnp.bfloat16)

    def value_block(distance):
        deq = v_scale[None] * codes[distance][1].astype(jnp.float32) - v_offset[None]
        return jnp.einsum("tkd,de->tke", deq, hadamard, precision=lax.Precision.HIGHEST).astype(
            jnp.bfloat16
        )

    keys = [key_block(distance) for distance in range(reach + 1)]
    values = [value_block(distance) for distance in range(reach + 1)]
    queries = query.reshape(block_rows, kv_heads, group, head_size)
    upstream_rows = grad_out.reshape(block_rows, kv_heads, group, head_size)
    delta = jnp.sum(grad_out.astype(jnp.float32) * out_forward.astype(jnp.float32), axis=-1)
    delta = jnp.transpose(delta.reshape(block_rows, kv_heads, group), (1, 2, 0))
    row_index = jnp.arange(block_rows, dtype=jnp.int32)[:, None]
    col_index = jnp.arange(block_rows, dtype=jnp.int32)[None, :]
    masks = []
    for distance in range(reach + 1):
        gap = distance * block_rows + row_index - col_index
        masks.append((gap >= 0) & (gap < WIN) & (device_block >= distance))

    def block_scores(distance):
        return (
            jnp.einsum("tkgd,ukd->kgtu", queries, keys[distance], preferred_element_type=jnp.float32)
            * scale
        )

    first = block_scores(0)
    top = jnp.max(jnp.where(masks[0], first, -jnp.inf), axis=-1)
    total = jnp.sum(jnp.where(masks[0], jnp.exp(first - top[..., None]), 0.0), axis=-1)
    for distance in range(1, reach + 1):
        scores = block_scores(distance)
        raised = jnp.maximum(top, jnp.max(jnp.where(masks[distance], scores, -jnp.inf), axis=-1))
        total = total * jnp.exp(top - raised) + jnp.sum(
            jnp.where(masks[distance], jnp.exp(scores - raised[..., None]), 0.0), axis=-1
        )
        top = raised
    log_total = top + jnp.log(total)
    query_acc = jnp.zeros((block_rows, kv_heads, group, head_size), jnp.float32)
    parts = [None] * (reach + 1)
    local_terms = 0.0
    for distance in reversed(range(reach + 1)):
        scores = block_scores(distance)
        weights = jnp.where(masks[distance], jnp.exp(scores - log_total[..., None]), 0.0)
        weights_low = weights.astype(jnp.bfloat16)
        upstream = jnp.einsum(
            "tkgd,ukd->kgtu", upstream_rows, values[distance], preferred_element_type=jnp.float32
        )
        score_grad = (weights * (upstream - delta[..., None])).astype(jnp.bfloat16)
        query_acc = query_acc + jnp.einsum(
            "kgtu,ukd->tkgd", score_grad, keys[distance], preferred_element_type=jnp.float32
        )
        key_part = (
            jnp.einsum("kgtu,tkgd->ukd", score_grad, queries, preferred_element_type=jnp.float32)
            * scale
        )
        value_part = jnp.einsum(
            "kgtu,tkgd->ukd", weights_low, upstream_rows, preferred_element_type=jnp.float32
        )
        parts[distance] = jnp.stack([key_part, value_part])
        key_deq_part = rotate_back(key_part, *tables[distance])
        value_deq_part = jnp.einsum(
            "tke,de->tkd", value_part, hadamard, precision=lax.Precision.HIGHEST
        )
        local_terms = local_terms + jnp.stack(
            [
                jnp.sum(key_deq_part * codes[distance][0].astype(jnp.float32), axis=0),
                -jnp.sum(key_deq_part, axis=0),
                jnp.sum(value_deq_part * codes[distance][1].astype(jnp.float32), axis=0),
                -jnp.sum(value_deq_part, axis=0),
            ]
        )

    back = shift(jnp.stack([parts[3], parts[4]]).astype(jnp.bfloat16), -2)
    column = jnp.sum(gather_all(local_terms, "z"), axis=0)
    near = (parts[1] + back[0].astype(jnp.float32)).astype(jnp.bfloat16)
    next_near = (parts[2] + back[1].astype(jnp.float32)).astype(jnp.bfloat16)
    near = shift(near, -1)
    next_near = shift(next_near, -2)
    columns = gather_all(column, FLAT)
    columns = jnp.sum(columns.reshape((lax.axis_size("head"), -1) + column.shape), axis=1)
    squares = jnp.sum(columns * columns)
    summed = lax.dynamic_index_in_dim(columns, lax.axis_index("head"), 0, keepdims=False)
    quant_grads = summed * jnp.minimum(1.0, clip_limit / jnp.sqrt(squares + 1e-06))

    collected = parts[0] + near.astype(jnp.float32) + next_near.astype(jnp.float32)
    key_deq_grad = rotate_back(collected[0], *tables[0])
    value_deq_grad = jnp.einsum(
        "tke,de->tkd", collected[1], hadamard, precision=lax.Precision.HIGHEST
    )
    key_grad = jnp.where((k_codes > 0) & (k_codes < 15), key_deq_grad, 0.0).astype(jnp.bfloat16)
    value_grad = jnp.where((v_codes > 0) & (v_codes < 15), value_deq_grad, 0.0).astype(jnp.bfloat16)
    query_grad = (
        (query_acc * scale).reshape(block_rows, query_heads, head_size).astype(jnp.bfloat16)
    )
    return (query_grad, key_grad, value_grad, quant_grads)


def solution(mesh):
    sizes = (mesh.shape["head"], mesh.shape["outer"] // 2, 2, 2, mesh.shape["inner"] // 2)
    split = Mesh(mesh.devices.reshape(sizes), ("head",) + TOK)
    rows = P(TOK, "head", None)
    steps = P("head", None)
    return jax.shard_map(
        body,
        mesh=split,
        in_specs=(rows, rows, rows, rows, steps, steps, rows, steps, steps),
        out_specs=(rows, rows, rows, P(None, "head", None)),
        check_vma=False,
    )
```

```python
import math

import jax
import jax.numpy as jnp
from jax import lax
from jax.experimental import pallas as pl
from jax.experimental.pallas import tpu as pltpu
from jax.sharding import Mesh, PartitionSpec as P

WIN = 512
ROWS = 128
HEAD = 128
QUERY_HEADS = 16
KV_HEADS = 2
BLOCKS = WIN // ROWS + 1
SPAN = BLOCKS * ROWS
WIDE = KV_HEADS * HEAD
CHUNK = 32
COLS = CHUNK * QUERY_HEADS
REACH = WIN + CHUNK
CHUNKS = ROWS // CHUNK
SCALE = 1.0 / math.sqrt(HEAD)
FLOOR = -3.0e38
clip_limit = 16.0
rope_base = 500000.0
TOK = ("x", "core", "ylo", "z")
FLAT = ("head", "x", "core", "ylo")
F32 = jnp.float32
BF16 = jnp.bfloat16


def shift(value, by):
    count = 1
    for axis in TOK:
        count *= lax.axis_size(axis)
    pairs = [(i, i + by) for i in range(count) if 0 <= i + by < count]
    return lax.ppermute(value, TOK, pairs)


def axis_count(axes):
    count = 1
    for axis in axes:
        count *= lax.axis_size(axis)
    return count


def split_two(value):
    high = value.astype(BF16)
    return high, (value - high.astype(F32)).astype(BF16)


def split_three(value):
    high = value.astype(BF16)
    rest = value - high.astype(F32)
    middle = rest.astype(BF16)
    return high, middle, (rest - middle.astype(F32)).astype(BF16)


def matmul(left, right):
    return jnp.dot(left, right, preferred_element_type=F32)


def matmul_nt(left, right):
    return lax.dot_general(left, right, (((1,), (1,)), ((), ())), preferred_element_type=F32)


def head_cols(head):
    return slice(head * HEAD, (head + 1) * HEAD)


def pack_kernel(key_ref, value_ref, out_ref):
    for head in range(KV_HEADS):
        picked = pl.ds(head, ROWS, stride=KV_HEADS)
        out_ref[:, head_cols(head)] = key_ref[picked, :].astype(F32).astype(BF16)
        out_ref[:, head_cols(KV_HEADS + head)] = value_ref[picked, :].astype(F32).astype(BF16)


def delta_kernel(grad_ref, forward_ref, out_ref):
    ones = jnp.ones((8, HEAD), BF16)
    product = grad_ref[...].astype(F32) * forward_ref[...].astype(F32)
    total = 0.0
    for piece in split_three(product):
        total = total + matmul_nt(ones, piece)
    out_ref[...] = total


def widen(rows, low):
    zero = jnp.zeros_like(rows)
    return jnp.concatenate([jnp.where(low, rows, zero), jnp.where(low, zero, rows)], axis=1)


def main_kernel(
    place_ref,
    query_ref,
    grad_ref,
    delta_ref,
    code4,
    code3,
    code2,
    code1,
    code0,
    cos_ref,
    sin_ref,
    steps_ref,
    had_ref,
    far4_ref,
    far3_ref,
    mid2_ref,
    near1_ref,
    own0_ref,
    query_out,
    raw_ref,
    keys,
    keys_t,
    values,
    wide_q,
    wide_g,
    scores,
    grads,
    key_acc,
    value_acc,
):
    code_refs = (code4, code3, code2, code1, code0)
    hadamard = had_ref[...]
    for block in range(BLOCKS):
        rows = slice(block * ROWS, (block + 1) * ROWS)
        cosines, sines = cos_ref[rows, :], sin_ref[rows, :]
        for head in range(KV_HEADS):
            cols = head_cols(head)
            code = code_refs[block][:, cols].astype(F32)
            deq = steps_ref[0:1, cols] * code - steps_ref[1:2, cols]
            turned = deq * cosines + pltpu.roll(deq, HEAD // 2, 1) * sines
            keys[rows, cols] = turned.astype(BF16)
            keys_t[cols, rows] = turned.T.astype(BF16)
            code = code_refs[block][:, head_cols(KV_HEADS + head)].astype(F32)
            deq = steps_ref[2:3, cols] * code - steps_ref[3:4, cols]
            total = 0.0
            for piece in split_three(deq):
                total = total + matmul(piece, hadamard)
            values[rows, cols] = (total * SCALE).astype(BF16)
    low = lax.broadcasted_iota(jnp.int32, (COLS, HEAD), 0) % QUERY_HEADS < QUERY_HEADS // KV_HEADS
    edge_row = lax.broadcasted_iota(jnp.int32, (CHUNK, COLS), 0)
    edge_token = lax.broadcasted_iota(jnp.int32, (CHUNK, COLS), 1) // QUERY_HEADS
    for chunk in range(CHUNKS):
        picked = slice(chunk * COLS, (chunk + 1) * COLS)
        span = slice(chunk * CHUNK, chunk * CHUNK + REACH)
        wide_q[picked, :] = widen(query_ref[picked, :], low)
        wide_g[picked, :] = widen(grad_ref[picked, :], low)
        score = matmul_nt(keys[span, :], wide_q[picked, :])
        scores[chunk, :CHUNK, :] = jnp.where(edge_row > edge_token, score[:CHUNK], FLOOR)
        scores[chunk, CHUNK:WIN, :] = score[CHUNK:WIN]
        scores[chunk, WIN:, :] = jnp.where(edge_row <= edge_token, score[WIN:], FLOOR)

    missing = WIN - place_ref[0] * ROWS

    @pl.when(missing > 0)
    def _():
        row = lax.broadcasted_iota(jnp.int32, (REACH, COLS), 0)
        for chunk in range(CHUNKS):
            scores[chunk] = jnp.where(row + chunk * CHUNK < missing, FLOOR, scores[chunk])

    key_acc[...] = jnp.zeros_like(key_acc)
    value_acc[...] = jnp.zeros_like(value_acc)
    grads[...] = jnp.zeros_like(grads)
    low_lane = (
        lax.broadcasted_iota(jnp.int32, (HEAD, COLS), 1) % QUERY_HEADS < QUERY_HEADS // KV_HEADS
    )
    for chunk in range(CHUNKS):
        picked = slice(chunk * COLS, (chunk + 1) * COLS)
        span = slice(chunk * CHUNK, chunk * CHUNK + REACH)
        score = scores[chunk]
        top = jnp.max(score, axis=0, keepdims=True)
        weights = jnp.exp((score - top) * SCALE)
        weights = weights * (1.0 / jnp.sum(weights, axis=0, keepdims=True))
        upstream = matmul_nt(values[span, :], wide_g[picked, :])
        grad = (weights * (upstream - delta_ref[0:1, picked])).astype(BF16)
        grads[chunk, span, :] = grad
        value_acc[span, :] += matmul(weights.astype(BF16), wide_g[picked, :])
        key_acc[span, :] += matmul(grad, wide_q[picked, :])
        both = matmul(keys_t[...], grads[chunk])
        query_grad = jnp.where(low_lane, both[:HEAD], both[HEAD:]) * SCALE
        query_out[picked, :] = query_grad.T.astype(BF16)

    outs = (far4_ref, far3_ref, mid2_ref, near1_ref, own0_ref)
    for head in range(KV_HEADS):
        cols = head_cols(head)
        value_cols = head_cols(KV_HEADS + head)
        sums = [0.0, 0.0, 0.0, 0.0]
        for block in range(BLOCKS):
            rows = slice(block * ROWS, (block + 1) * ROWS)
            part = key_acc[rows, cols] * SCALE
            part = part * cos_ref[rows, :] - pltpu.roll(part, HEAD // 2, 1) * sin_ref[rows, :]
            outs[block][:, cols] = part.astype(outs[block].dtype)
            code = code_refs[block][:, cols].astype(F32)
            sums[0] = sums[0] + jnp.sum(part * code, axis=0, keepdims=True)
            sums[1] = sums[1] - jnp.sum(part, axis=0, keepdims=True)
            total = 0.0
            for piece in split_three(value_acc[rows, cols]):
                total = total + matmul(piece, hadamard)
            part = total * SCALE
            outs[block][:, value_cols] = part.astype(outs[block].dtype)
            code = code_refs[block][:, value_cols].astype(F32)
            sums[2] = sums[2] + jnp.sum(part * code, axis=0, keepdims=True)
            sums[3] = sums[3] - jnp.sum(part, axis=0, keepdims=True)
        for term in range(4):
            row = term * KV_HEADS + head
            for copy in range(raw_ref.shape[0]):
                raw_ref[copy, row : row + 1, :] = sums[term]


def spread_kernel(in_ref, out_ref):
    total = jnp.sum(in_ref[...], axis=0)
    out_ref[...] = jnp.broadcast_to(total[None], out_ref.shape)


def finish_kernel(
    place_ref, all_ref, own_ref, near_ref, mid_ref, code_ref, key_out, value_out, quant_out, rows_ref
):
    per_head = all_ref.shape[0] // 2
    first = jnp.sum(all_ref[:per_head], axis=0)
    second = jnp.sum(all_ref[per_head:], axis=0)
    squares = jnp.sum(first * first + second * second, keepdims=True)
    mine = jnp.where(place_ref[1] == 0, first, second)
    quant_out[...] = mine * jnp.minimum(1.0, clip_limit / jnp.sqrt(squares + 1e-06))
    total = own_ref[...] + near_ref[...].astype(F32) + mid_ref[...].astype(F32)
    code = code_ref[...].astype(F32)
    total = jnp.where((code > 0.0) & (code < 15.0), total, 0.0)
    for kind, out in enumerate((key_out, value_out)):
        for head in range(KV_HEADS):
            rows_ref[pl.ds(head, ROWS, stride=KV_HEADS), :] = total[
                :, head_cols(kind * KV_HEADS + head)
            ]
        out[...] = rows_ref[...].astype(BF16)


def call(kernel, outs, scratch=(), scalars=0, inputs=0, limit=32, cost=None):
    specs = [pl.BlockSpec(memory_space=pltpu.SMEM)] * scalars
    specs = specs + [pl.BlockSpec(memory_space=pltpu.VMEM)] * inputs
    return pl.pallas_call(
        kernel,
        out_shape=[jax.ShapeDtypeStruct(shape, dtype) for shape, dtype in outs],
        in_specs=specs,
        out_specs=[pl.BlockSpec(memory_space=pltpu.VMEM)] * len(outs),
        scratch_shapes=[pltpu.VMEM(shape, dtype) for shape, dtype in scratch],
        compiler_params=pltpu.CompilerParams(vmem_limit_bytes=limit * 1024 * 1024),
        cost_estimate=cost,
    )


def rope_tables(positions, head_size):
    freqs = rope_base ** (-jnp.arange(0, head_size, 2, dtype=jnp.float32) / head_size)
    angles = positions.astype(jnp.float32)[:, None] * freqs[None, :]
    cosines, sines = jnp.cos(angles), jnp.sin(angles)
    return (
        jnp.concatenate([cosines, cosines], axis=-1),
        jnp.concatenate([-sines, sines], axis=-1),
    )


def hadamard_signs(order):
    index = jnp.arange(order, dtype=jnp.int32)
    common = jnp.bitwise_and(index[:, None], index[None, :])
    parity = jnp.zeros((order, order), jnp.int32)
    for level in range(order.bit_length() - 1):
        parity = parity + jnp.bitwise_and(jnp.right_shift(common, level), 1)
    return (1 - 2 * (parity % 2)).astype(BF16)


def body(query, grad_out, out_forward, k_codes, k_scale, k_offset, v_codes, v_scale, v_offset):
    device_block = jnp.int32(0)
    for axis in TOK:
        device_block = device_block * lax.axis_size(axis) + lax.axis_index(axis)
    place = jnp.stack([device_block, lax.axis_index("head")]).astype(jnp.int32)
    flat_codes = (KV_HEADS * ROWS, HEAD)
    flat_rows = (QUERY_HEADS * ROWS, HEAD)
    pack = (ROWS, 2 * WIDE)

    (own,) = call(pack_kernel, [(pack, BF16)], inputs=2)(
        k_codes.reshape(flat_codes), v_codes.reshape(flat_codes)
    )
    two = shift(own, 2)
    one = shift(own, 1)
    queries = query.reshape(flat_rows)
    upstream_rows = grad_out.reshape(flat_rows)
    (delta,) = call(delta_kernel, [((8, QUERY_HEADS * ROWS), F32)], inputs=2)(
        upstream_rows, out_forward.reshape(flat_rows)
    )
    first_row = device_block * ROWS - WIN
    cosines, sines = rope_tables(first_row + jnp.arange(SPAN, dtype=jnp.int32), HEAD)
    steps = jnp.stack([k_scale, k_offset, v_scale, v_offset]).reshape(4, WIDE)
    hadamard = hadamard_signs(HEAD)
    four = shift(two, 2)
    three = shift(two, 1)

    column = axis_count(("z",))
    far4, far3, mid2, near1, own0, query_grad, raw = call(
        main_kernel,
        [
            (pack, BF16),
            (pack, BF16),
            (pack, F32),
            (pack, BF16),
            (pack, F32),
            (flat_rows, BF16),
            ((column, 4 * KV_HEADS, HEAD), F32),
        ],
        scratch=[
            ((SPAN, WIDE), BF16),
            ((WIDE, SPAN), BF16),
            ((SPAN, WIDE), BF16),
            ((QUERY_HEADS * ROWS, WIDE), BF16),
            ((QUERY_HEADS * ROWS, WIDE), BF16),
            ((CHUNKS, REACH, COLS), F32),
            ((CHUNKS, SPAN, COLS), BF16),
            ((SPAN, WIDE), F32),
            ((SPAN, WIDE), F32),
        ],
        scalars=1,
        inputs=12,
    )(place, queries, upstream_rows, delta, four, three, two, one, own, cosines, sines, steps, hadamard)

    from4 = shift(far4, -2)
    from3 = shift(far3, -1)
    from1 = shift(near1, -1)
    raw = lax.all_to_all(raw, "z", 0, 0)
    (raw,) = call(
        spread_kernel, [((axis_count(FLAT), 4 * KV_HEADS, HEAD), F32)], inputs=1
    )(raw)
    mid = (mid2 + from4.astype(F32) + from3.astype(F32)).astype(BF16)
    from2 = shift(mid, -2)
    raw = lax.all_to_all(raw, FLAT, 0, 0)
    key_grad, value_grad, quant = call(
        finish_kernel,
        [(flat_codes, BF16), (flat_codes, BF16), ((4 * KV_HEADS, HEAD), F32)],
        scratch=[(flat_codes, F32)],
        scalars=1,
        inputs=5,
    )(place, raw, own0, from1, from2, own)
    return (
        query_grad.reshape(ROWS, QUERY_HEADS, HEAD),
        key_grad.reshape(ROWS, KV_HEADS, HEAD),
        value_grad.reshape(ROWS, KV_HEADS, HEAD),
        quant.reshape(4, KV_HEADS, HEAD),
    )


def solution(mesh):
    sizes = (mesh.shape["head"], mesh.shape["outer"] // 2, 2, 2, mesh.shape["inner"] // 2)
    split = Mesh(mesh.devices.reshape(sizes), ("head",) + TOK)
    rows = P(TOK, "head", None)
    steps = P("head", None)
    return jax.shard_map(
        body,
        mesh=split,
        in_specs=(rows, rows, rows, rows, steps, steps, rows, steps, steps),
        out_specs=(rows, rows, rows, P(None, "head", None)),
        check_vma=False,
    )
```

```python
import math

import jax
import jax.numpy as jnp
from jax import lax
from jax.experimental import pallas as pl
from jax.experimental.pallas import tpu as pltpu
from jax.sharding import Mesh, PartitionSpec as P

WIN = 512
ROWS = 128
HEAD = 128
QUERY_HEADS = 16
KV_HEADS = 2
BLOCKS = WIN // ROWS + 1
SPAN = BLOCKS * ROWS
WIDE = KV_HEADS * HEAD
CHUNK = 32
COLS = CHUNK * QUERY_HEADS
CHUNKS = ROWS // CHUNK
FAR_BLOCKS = 2
PIECES = 4
FINISH_FLOPS = None
MIDDLE_FLOPS = 3 * 10**9
FAR_ROWS = FAR_BLOCKS * ROWS
NEAR_ROWS = SPAN - FAR_ROWS
SCALE = 1.0 / math.sqrt(HEAD)
FLOOR = -3.0e38
clip_limit = 16.0
rope_base = 500000.0
TOK = ("x", "core", "ylo", "z")
FLAT = ("head", "x", "core", "ylo")
F32 = jnp.float32
BF16 = jnp.bfloat16


def shift(value, by):
    count = 1
    for axis in TOK:
        count *= lax.axis_size(axis)
    pairs = [(i, i + by) for i in range(count) if 0 <= i + by < count]
    return lax.ppermute(value, TOK, pairs)


def axis_count(axes):
    count = 1
    for axis in axes:
        count *= lax.axis_size(axis)
    return count


def split_two(value):
    high = value.astype(BF16)
    return high, (value - high.astype(F32)).astype(BF16)


def split_three(value):
    high = value.astype(BF16)
    rest = value - high.astype(F32)
    middle = rest.astype(BF16)
    return high, middle, (rest - middle.astype(F32)).astype(BF16)


def matmul(left, right):
    return jnp.dot(left, right, preferred_element_type=F32)


def matmul_nt(left, right):
    return lax.dot_general(left, right, (((1,), (1,)), ((), ())), preferred_element_type=F32)


def head_cols(head):
    return slice(head * HEAD, (head + 1) * HEAD)


def pack_kernel(key_hbm, value_hbm, out_ref, rows_ref, sems):
    copies = []
    step = KV_HEADS * ROWS // PIECES
    for kind, source in enumerate((key_hbm, value_hbm)):
        for piece in range(PIECES):
            rows = pl.ds(piece * step, step)
            copies.append(
                pltpu.make_async_copy(
                    source.at[rows], rows_ref.at[kind, rows], sems.at[kind * PIECES + piece]
                )
            )
            copies[-1].start()
    for kind in range(2):
        for piece in range(PIECES):
            copies[kind * PIECES + piece].wait()
        for head in range(KV_HEADS):
            code = rows_ref[kind, pl.ds(head, ROWS, stride=KV_HEADS), :].astype(F32)
            out_ref[:, head_cols(kind * KV_HEADS + head)] = code.astype(BF16)


def widen(rows, low):
    zero = jnp.zeros_like(rows)
    return jnp.concatenate([jnp.where(low, rows, zero), jnp.where(low, zero, rows)], axis=1)


def dequantize(code_ref, tables, block, steps_ref, hadamard):
    rows = slice(block * ROWS, (block + 1) * ROWS)
    cos_ref, sin_ref = tables
    cosines, sines = cos_ref[rows, :], sin_ref[rows, :]
    keys, values = [], []
    for head in range(KV_HEADS):
        cols = head_cols(head)
        code = code_ref[:, cols].astype(F32)
        deq = steps_ref[0:1, cols] * code - steps_ref[1:2, cols]
        keys.append(deq * cosines + pltpu.roll(deq, HEAD // 2, 1) * sines)
        code = code_ref[:, head_cols(KV_HEADS + head)].astype(F32)
        deq = steps_ref[2:3, cols] * code - steps_ref[3:4, cols]
        total = 0.0
        for piece in split_three(deq):
            total = total + matmul(piece, hadamard)
        values.append((total * SCALE).astype(BF16))
    return keys, values


def store_block(dequantized, row, keys, keys_t, values):
    rows = slice(row, row + ROWS)
    for head in range(KV_HEADS):
        cols = head_cols(head)
        keys[rows, cols] = dequantized[0][head].astype(BF16)
        keys_t[cols, rows] = dequantized[0][head].T.astype(BF16)
        values[rows, cols] = dequantized[1][head]


def near_kernel(
    place_ref,
    query_ref,
    grad_ref,
    forward_ref,
    code2,
    code1,
    code0,
    cos_ref,
    sin_ref,
    steps_ref,
    had_ref,
    wide_q,
    wide_g,
    keys_t,
    near_p,
    near_u,
    stats,
    keys,
    values,
    scores,
):
    hadamard = had_ref[...]
    tables = (cos_ref, sin_ref)
    for block, code_ref in enumerate((code2, code1, code0)):
        made = dequantize(code_ref, tables, FAR_BLOCKS + block, steps_ref, hadamard)
        store_block(made, block * ROWS, keys, keys_t, values)
    low = lax.broadcasted_iota(jnp.int32, (COLS, HEAD), 0) % QUERY_HEADS < QUERY_HEADS // KV_HEADS
    edge_row = lax.broadcasted_iota(jnp.int32, (CHUNK, COLS), 0)
    edge_token = lax.broadcasted_iota(jnp.int32, (CHUNK, COLS), 1) // QUERY_HEADS
    for chunk in range(CHUNKS):
        picked = slice(chunk * COLS, (chunk + 1) * COLS)
        count = NEAR_ROWS - ROWS + (chunk + 1) * CHUNK
        wide_q[picked, :] = widen(query_ref[picked, :], low)
        wide_g[picked, :] = widen(grad_ref[picked, :], low)
        score = matmul_nt(keys[:count, :], wide_q[picked, :])
        last = count - CHUNK
        scores[chunk, :last, :] = score[:last]
        scores[chunk, last:count, :] = jnp.where(edge_row <= edge_token, score[last:], FLOOR)

    missing = (BLOCKS - FAR_BLOCKS - 1 - place_ref[0]) * ROWS

    @pl.when(missing > 0)
    def _():
        row = lax.broadcasted_iota(jnp.int32, (NEAR_ROWS, COLS), 0)
        for chunk in range(CHUNKS):
            scores[chunk] = jnp.where(row < missing, FLOOR, scores[chunk])

    ones = jnp.ones((8, HEAD), BF16)
    for chunk in range(CHUNKS):
        picked = slice(chunk * COLS, (chunk + 1) * COLS)
        count = NEAR_ROWS - ROWS + (chunk + 1) * CHUNK
        delta = 0.0
        for piece in split_three(
            grad_ref[picked, :].astype(F32) * forward_ref[picked, :].astype(F32)
        ):
            delta = delta + matmul_nt(ones, piece)
        score = scores[chunk, :count, :]
        top = jnp.max(score, axis=0, keepdims=True)
        weights = jnp.exp((score - top) * SCALE)
        near_p[chunk, :count, :] = weights
        stats[0:1, picked] = top
        stats[1:2, picked] = jnp.sum(weights, axis=0, keepdims=True)
        stats[2:3, picked] = delta[0:1]
        near_u[chunk, :count, :] = matmul_nt(values[:count, :], wide_g[picked, :]) - delta[0:1]


def far_kernel(
    place_ref,
    code4,
    code3,
    code2,
    code1,
    code0,
    cos_ref,
    sin_ref,
    steps_ref,
    had_ref,
    wide_q,
    wide_g,
    near_p,
    near_u,
    stats,
    near_t,
    raw_ref,
    four_out,
    odd_out,
    parts,
    query_hbm,
    keys,
    keys_t,
    values,
    scores,
    lows,
    key_acc,
    value_acc,
    grads,
    query_out,
    sems,
):
    hadamard = had_ref[...]
    tables = (cos_ref, sin_ref)
    for block, code_ref in enumerate((code4, code3)):
        made = dequantize(code_ref, tables, block, steps_ref, hadamard)
        store_block(made, block * ROWS, keys, keys_t, values)
    edge_row = lax.broadcasted_iota(jnp.int32, (CHUNK, COLS), 0)
    edge_token = lax.broadcasted_iota(jnp.int32, (CHUNK, COLS), 1) // QUERY_HEADS
    for chunk in range(CHUNKS):
        picked = slice(chunk * COLS, (chunk + 1) * COLS)
        first = chunk * CHUNK
        score = matmul_nt(keys[first:, :], wide_q[picked, :])
        scores[chunk, first : first + CHUNK, :] = jnp.where(
            edge_row > edge_token, score[:CHUNK], FLOOR
        )
        scores[chunk, first + CHUNK :, :] = score[CHUNK:]

    missing = WIN - place_ref[0] * ROWS

    @pl.when(missing > 0)
    def _():
        row = lax.broadcasted_iota(jnp.int32, (FAR_ROWS, COLS), 0)
        for chunk in range(CHUNKS):
            scores[chunk] = jnp.where(row < missing, FLOOR, scores[chunk])

    key_acc[...] = jnp.zeros_like(key_acc)
    value_acc[...] = jnp.zeros_like(value_acc)
    grads[...] = jnp.zeros_like(grads)
    low_lane = (
        lax.broadcasted_iota(jnp.int32, (HEAD, COLS), 1) % QUERY_HEADS < QUERY_HEADS // KV_HEADS
    )
    copies = []
    for chunk in range(CHUNKS):
        picked = slice(chunk * COLS, (chunk + 1) * COLS)
        first = chunk * CHUNK
        count = NEAR_ROWS - ROWS + (chunk + 1) * CHUNK
        last = FAR_ROWS + count
        score = scores[chunk, first:, :]
        near_top = stats[0:1, picked]
        top = jnp.maximum(near_top, jnp.max(score, axis=0, keepdims=True))
        far = jnp.exp((score - top) * SCALE)
        kept = jnp.exp((near_top - top) * SCALE)
        inverse = 1.0 / (stats[1:2, picked] * kept + jnp.sum(far, axis=0, keepdims=True))
        far = far * inverse
        near = near_p[chunk, :count, :] * (kept * inverse)
        upstream = matmul_nt(values[first:, :], wide_g[picked, :]) - stats[2:3, picked]
        lows[chunk, first:FAR_ROWS, :] = far.astype(BF16)
        lows[chunk, FAR_ROWS:last, :] = near.astype(BF16)
        grads[chunk, first:FAR_ROWS, :] = (far * upstream).astype(BF16)
        grads[chunk, FAR_ROWS:last, :] = (near * near_u[chunk, :count, :]).astype(BF16)
        value_acc[first:last, :] += matmul(lows[chunk, first:last, :], wide_g[picked, :])
        key_acc[first:last, :] += matmul(grads[chunk, first:last, :], wide_q[picked, :])
        both = matmul(keys_t[...], grads[chunk, :FAR_ROWS, :])
        both = both + matmul(near_t[...], grads[chunk, FAR_ROWS:, :])
        query_grad = jnp.where(low_lane, both[:HEAD], both[HEAD:]) * SCALE
        query_out[picked, :] = query_grad.T.astype(BF16)
        rows = pl.ds(chunk * COLS, COLS)
        copies.append(
            pltpu.make_async_copy(query_out.at[rows], query_hbm.at[rows], sems.at[chunk])
        )
        copies[-1].start()

    code_refs = (code4, code3, code2, code1, code0)
    outs = (
        four_out,
        odd_out.at[:ROWS],
        parts.at[:ROWS],
        odd_out.at[ROWS:],
        parts.at[ROWS:],
    )
    for head in range(KV_HEADS):
        cols = head_cols(head)
        value_cols = head_cols(KV_HEADS + head)
        sums = [0.0, 0.0, 0.0, 0.0]
        for block in range(BLOCKS):
            rows = slice(block * ROWS, (block + 1) * ROWS)
            out = outs[block]
            part = key_acc[rows, cols] * SCALE
            part = part * cos_ref[rows, :] - pltpu.roll(part, HEAD // 2, 1) * sin_ref[rows, :]
            out[:, cols] = part.astype(out.dtype)
            code = code_refs[block][:, cols].astype(F32)
            sums[0] = sums[0] + jnp.sum(part * code, axis=0, keepdims=True)
            sums[1] = sums[1] - jnp.sum(part, axis=0, keepdims=True)
            total = 0.0
            for piece in split_two(value_acc[rows, cols]):
                total = total + matmul(piece, hadamard)
            part = total * SCALE
            out[:, value_cols] = part.astype(out.dtype)
            code = code_refs[block][:, value_cols].astype(F32)
            sums[2] = sums[2] + jnp.sum(part * code, axis=0, keepdims=True)
            sums[3] = sums[3] - jnp.sum(part, axis=0, keepdims=True)
        for term in range(4):
            row = term * KV_HEADS + head
            for copy in range(raw_ref.shape[0]):
                raw_ref[copy, row : row + 1, :] = sums[term]
    for copy in copies:
        copy.wait()


def middle_kernel(parts, four_ref, odd_ref, mid_ref):
    total = parts[:ROWS, :] + four_ref[...].astype(F32) + odd_ref[:ROWS, :].astype(F32)
    mid_ref[...] = total.astype(BF16)


def spread_kernel(in_ref, raw_ref):
    per_head = in_ref.shape[0] // 2
    terms = 4 * KV_HEADS
    for head in range(2):
        total = jnp.sum(in_ref[head * per_head : (head + 1) * per_head], axis=0)
        shape = (raw_ref.shape[0], terms, HEAD)
        raw_ref[:, head * terms : (head + 1) * terms, :] = jnp.broadcast_to(total[None], shape)


def clip_kernel(first_ref, all_ref, quant_out):
    total = jnp.sum(all_ref[...], axis=0)
    squares = jnp.sum(total * total, keepdims=True)
    mine = jnp.where(first_ref[...] > 0.0, total[: 4 * KV_HEADS], total[4 * KV_HEADS :])
    quant_out[...] = mine * jnp.minimum(1.0, clip_limit / jnp.sqrt(squares + 1e-06))


def finish_kernel(first_ref, parts, odd_ref, mid_ref, code_ref, key_out, value_out, first_out, rows_ref):
    first_out[...] = first_ref[...]
    near = odd_ref[ROWS:, :].astype(F32)
    total = parts[ROWS:, :] + near + mid_ref[...].astype(F32)
    code = code_ref[...].astype(F32)
    total = jnp.where((code > 0.0) & (code < 15.0), total, 0.0)
    for kind, out in enumerate((key_out, value_out)):
        for head in range(KV_HEADS):
            rows_ref[kind, pl.ds(head, ROWS, stride=KV_HEADS), :] = total[
                :, head_cols(kind * KV_HEADS + head)
            ]
        out[...] = rows_ref[kind].astype(BF16)


def call(
    kernel, outs, scratch=(), scalars=0, inputs=(), hbm_outs=(), copies=0, limit=24, flops=None
):
    place = {"s": pltpu.SMEM, "v": pltpu.VMEM, "h": pl.ANY}
    specs = [pl.BlockSpec(memory_space=place[kind]) for kind in "s" * scalars + inputs]
    out_specs = [pl.BlockSpec(memory_space=pltpu.VMEM)] * len(outs)
    out_specs = out_specs + [pl.BlockSpec(memory_space=pltpu.HBM)] * len(hbm_outs)
    outs = list(outs) + list(hbm_outs)
    scratch_shapes = [pltpu.VMEM(shape, dtype) for shape, dtype in scratch]
    if copies:
        scratch_shapes.append(pltpu.SemaphoreType.DMA((copies,)))
    params, cost = {}, None
    if flops:
        cost = pl.CostEstimate(flops=flops, bytes_accessed=0, transcendentals=0)
    if limit:
        params["vmem_limit_bytes"] = limit * 1024 * 1024
    return pl.pallas_call(
        kernel,
        out_shape=[jax.ShapeDtypeStruct(shape, dtype) for shape, dtype in outs],
        in_specs=specs,
        out_specs=out_specs,
        scratch_shapes=scratch_shapes,
        compiler_params=pltpu.CompilerParams(**params),
        cost_estimate=cost,
    )


def rope_tables(positions, head_size):
    freqs = rope_base ** (-jnp.arange(0, head_size, 2, dtype=jnp.float32) / head_size)
    angles = positions.astype(jnp.float32)[:, None] * freqs[None, :]
    cosines, sines = jnp.cos(angles), jnp.sin(angles)
    return (
        jnp.concatenate([cosines, cosines], axis=-1),
        jnp.concatenate([-sines, sines], axis=-1),
    )


def hadamard_signs(order):
    index = jnp.arange(order, dtype=jnp.int32)
    common = jnp.bitwise_and(index[:, None], index[None, :])
    parity = jnp.zeros((order, order), jnp.int32)
    for level in range(order.bit_length() - 1):
        parity = parity + jnp.bitwise_and(jnp.right_shift(common, level), 1)
    return (1 - 2 * (parity % 2)).astype(BF16)


def body(query, grad_out, out_forward, k_codes, k_scale, k_offset, v_codes, v_scale, v_offset):
    device_block = jnp.int32(0)
    for axis in TOK:
        device_block = device_block * lax.axis_size(axis) + lax.axis_index(axis)
    place = device_block.astype(jnp.int32).reshape(1)
    flat_codes = (KV_HEADS * ROWS, HEAD)
    flat_rows = (QUERY_HEADS * ROWS, HEAD)
    pack = (ROWS, 2 * WIDE)

    (own,) = call(
        pack_kernel, [(pack, BF16)], [((2,) + flat_codes, jnp.int32)], inputs="hh", copies=2 * PIECES, limit=0
    )(k_codes.reshape(flat_codes), v_codes.reshape(flat_codes))
    two = shift(own, 2)
    one = shift(own, 1)
    queries = query.reshape(flat_rows)
    upstream_rows = grad_out.reshape(flat_rows)
    first_row = device_block * ROWS - WIN
    cosines, sines = rope_tables(first_row + jnp.arange(SPAN, dtype=jnp.int32), HEAD)
    steps = jnp.stack([k_scale, k_offset, v_scale, v_offset]).reshape(4, WIDE)
    hadamard = hadamard_signs(HEAD)
    four = shift(two, 2)
    three = shift(two, 1)

    wide = (QUERY_HEADS * ROWS, WIDE)
    near_pairs = (CHUNKS, NEAR_ROWS, COLS)
    wide_q, wide_g, near_t, near_p, near_u, stats = call(
        near_kernel,
        [
            (wide, BF16),
            (wide, BF16),
            ((WIDE, NEAR_ROWS), BF16),
            (near_pairs, F32),
            (near_pairs, F32),
            ((8, QUERY_HEADS * ROWS), F32),
        ],
        scratch=[
            ((NEAR_ROWS, WIDE), BF16),
            ((NEAR_ROWS, WIDE), BF16),
            (near_pairs, F32),
        ],
        scalars=1,
        inputs="v" * 10,
    )(
        place,
        queries,
        upstream_rows,
        out_forward.reshape(flat_rows),
        two,
        one,
        own,
        cosines,
        sines,
        steps,
        hadamard,
    )
    raw, four_part, odd_part, parts, query_grad = call(
        far_kernel,
        [
            ((axis_count(FLAT), 4 * KV_HEADS, HEAD), F32),
            (pack, BF16),
            ((2 * ROWS, 2 * WIDE), BF16),
            ((2 * ROWS, 2 * WIDE), F32),
        ],
        scratch=[
            ((FAR_ROWS, WIDE), BF16),
            ((WIDE, FAR_ROWS), BF16),
            ((FAR_ROWS, WIDE), BF16),
            ((CHUNKS, FAR_ROWS, COLS), F32),
            ((CHUNKS, SPAN, COLS), BF16),
            ((SPAN, WIDE), F32),
            ((SPAN, WIDE), F32),
            ((CHUNKS, SPAN, COLS), BF16),
            (flat_rows, BF16),
        ],
        scalars=1,
        inputs="v" * 15,
        hbm_outs=[(flat_rows, BF16)],
        copies=CHUNKS,
    )(
        place,
        four,
        three,
        two,
        one,
        own,
        cosines,
        sines,
        steps,
        hadamard,
        wide_q,
        wide_g,
        near_p,
        near_u,
        stats,
        near_t,
    )
    four_part = shift(four_part, -2)
    odd_part = shift(odd_part, -1)
    raw = lax.all_to_all(raw, FLAT, 0, 0)
    columns = axis_count(("z",))
    (raw,) = call(spread_kernel, [((columns, 8 * KV_HEADS, HEAD), F32)], inputs="v")(raw)
    (mid,) = call(middle_kernel, [(pack, BF16)], inputs="vvv", flops=MIDDLE_FLOPS)(
        parts, four_part, odd_part
    )
    mid = shift(mid, -2)
    raw = lax.all_to_all(raw, "z", 0, 0)
    first = jnp.where(lax.axis_index("head") == 0, jnp.ones((4 * KV_HEADS, HEAD), F32), 0.0)
    key_grad, value_grad, first = call(
        finish_kernel,
        [(flat_codes, BF16)] * 2 + [((4 * KV_HEADS, HEAD), F32)],
        scratch=[((2,) + flat_codes, F32)],
        inputs="vvvvv",
        flops=FINISH_FLOPS,
    )(first, parts, odd_part, mid, own)
    (quant,) = call(clip_kernel, [((4 * KV_HEADS, HEAD), F32)], inputs="vv")(first, raw)
    return (
        query_grad.reshape(ROWS, QUERY_HEADS, HEAD),
        key_grad.reshape(ROWS, KV_HEADS, HEAD),
        value_grad.reshape(ROWS, KV_HEADS, HEAD),
        quant.reshape(4, KV_HEADS, HEAD),
    )


def solution(mesh):
    sizes = (mesh.shape["head"], mesh.shape["outer"] // 2, 2, 2, mesh.shape["inner"] // 2)
    split = Mesh(mesh.devices.reshape(sizes), ("head",) + TOK)
    rows = P(TOK, "head", None)
    steps = P("head", None)
    return jax.shard_map(
        body,
        mesh=split,
        in_specs=(rows, rows, rows, rows, steps, steps, rows, steps, steps),
        out_specs=(rows, rows, rows, P(None, "head", None)),
        check_vma=False,
    )
```

```python
import math

import jax
import jax.numpy as jnp
from jax import lax
from jax.experimental import pallas as pl
from jax.experimental.pallas import tpu as pltpu
from jax.sharding import Mesh, PartitionSpec as P

WIN = 512
ROWS = 128
HEAD = 128
QUERY_HEADS = 16
KV_HEADS = 2
BLOCKS = WIN // ROWS + 1
SPAN = BLOCKS * ROWS
WIDE = KV_HEADS * HEAD
CHUNK = 32
COLS = CHUNK * QUERY_HEADS
CHUNKS = ROWS // CHUNK
FAR_BLOCKS = 2
PIECES = 4
PACK_LIMIT = 0
FINISH_FLOPS = None
ADD_FLOPS = None
MIDDLE_FLOPS = 2 * 10**9
FAR_ROWS = FAR_BLOCKS * ROWS
NEAR_ROWS = SPAN - FAR_ROWS
SCALE = 1.0 / math.sqrt(HEAD)
FLOOR = -3.0e38
clip_limit = 16.0
rope_base = 500000.0
TOK = ("x", "core", "ylo", "z")
FLAT = ("head", "x", "core", "ylo")
F32 = jnp.float32
BF16 = jnp.bfloat16


def shift(value, by):
    count = 1
    for axis in TOK:
        count *= lax.axis_size(axis)
    pairs = [(i, i + by) for i in range(count) if 0 <= i + by < count]
    return lax.ppermute(value, TOK, pairs)


def axis_count(axes):
    count = 1
    for axis in axes:
        count *= lax.axis_size(axis)
    return count


def split_two(value):
    high = value.astype(BF16)
    return high, (value - high.astype(F32)).astype(BF16)


def split_three(value):
    high = value.astype(BF16)
    rest = value - high.astype(F32)
    middle = rest.astype(BF16)
    return high, middle, (rest - middle.astype(F32)).astype(BF16)


def matmul(left, right):
    return jnp.dot(left, right, preferred_element_type=F32)


def matmul_nt(left, right):
    return lax.dot_general(left, right, (((1,), (1,)), ((), ())), preferred_element_type=F32)


def head_cols(head):
    return slice(head * HEAD, (head + 1) * HEAD)


def pack_kernel(key_hbm, value_hbm, out_ref, rows_ref, sems):
    copies = []
    step = KV_HEADS * ROWS // PIECES
    for kind, source in enumerate((key_hbm, value_hbm)):
        for piece in range(PIECES):
            rows = pl.ds(piece * step, step)
            copies.append(
                pltpu.make_async_copy(
                    source.at[rows], rows_ref.at[kind, rows], sems.at[kind * PIECES + piece]
                )
            )
            copies[-1].start()
    for kind in range(2):
        for piece in range(PIECES):
            copies[kind * PIECES + piece].wait()
        for head in range(KV_HEADS):
            code = rows_ref[kind, pl.ds(head, ROWS, stride=KV_HEADS), :].astype(F32)
            out_ref[:, head_cols(kind * KV_HEADS + head)] = code.astype(BF16)


def widen(rows, low):
    zero = jnp.zeros_like(rows)
    return jnp.concatenate([jnp.where(low, rows, zero), jnp.where(low, zero, rows)], axis=1)


def dequantize(code_ref, tables, block, steps_ref, hadamard):
    rows = slice(block * ROWS, (block + 1) * ROWS)
    cos_ref, sin_ref = tables
    cosines, sines = cos_ref[rows, :], sin_ref[rows, :]
    keys, values = [], []
    for head in range(KV_HEADS):
        cols = head_cols(head)
        code = code_ref[:, cols].astype(F32)
        deq = steps_ref[0:1, cols] * code - steps_ref[1:2, cols]
        keys.append(deq * cosines + pltpu.roll(deq, HEAD // 2, 1) * sines)
        code = code_ref[:, head_cols(KV_HEADS + head)].astype(F32)
        deq = steps_ref[2:3, cols] * code - steps_ref[3:4, cols]
        total = 0.0
        for piece in split_three(deq):
            total = total + matmul(piece, hadamard)
        values.append((total * SCALE).astype(BF16))
    return keys, values


def store_block(dequantized, row, keys, keys_t, values):
    rows = slice(row, row + ROWS)
    for head in range(KV_HEADS):
        cols = head_cols(head)
        keys[rows, cols] = dequantized[0][head].astype(BF16)
        keys_t[cols, rows] = dequantized[0][head].T.astype(BF16)
        values[rows, cols] = dequantized[1][head]


def near_kernel(
    place_ref,
    query_ref,
    grad_ref,
    forward_ref,
    code2,
    code1,
    code0,
    cos_ref,
    sin_ref,
    steps_ref,
    had_ref,
    wide_q,
    wide_g,
    keys_t,
    near_p,
    near_u,
    stats,
    keys,
    values,
    scores,
):
    hadamard = had_ref[...]
    tables = (cos_ref, sin_ref)
    for block, code_ref in enumerate((code2, code1, code0)):
        made = dequantize(code_ref, tables, FAR_BLOCKS + block, steps_ref, hadamard)
        store_block(made, block * ROWS, keys, keys_t, values)
    low = lax.broadcasted_iota(jnp.int32, (COLS, HEAD), 0) % QUERY_HEADS < QUERY_HEADS // KV_HEADS
    edge_row = lax.broadcasted_iota(jnp.int32, (CHUNK, COLS), 0)
    edge_token = lax.broadcasted_iota(jnp.int32, (CHUNK, COLS), 1) // QUERY_HEADS
    for chunk in range(CHUNKS):
        picked = slice(chunk * COLS, (chunk + 1) * COLS)
        count = NEAR_ROWS - ROWS + (chunk + 1) * CHUNK
        wide_q[picked, :] = widen(query_ref[picked, :], low)
        wide_g[picked, :] = widen(grad_ref[picked, :], low)
        score = matmul_nt(keys[:count, :], wide_q[picked, :])
        last = count - CHUNK
        scores[chunk, :last, :] = score[:last]
        scores[chunk, last:count, :] = jnp.where(edge_row <= edge_token, score[last:], FLOOR)

    missing = (BLOCKS - FAR_BLOCKS - 1 - place_ref[0]) * ROWS

    @pl.when(missing > 0)
    def _():
        row = lax.broadcasted_iota(jnp.int32, (NEAR_ROWS, COLS), 0)
        for chunk in range(CHUNKS):
            scores[chunk] = jnp.where(row < missing, FLOOR, scores[chunk])

    ones = jnp.ones((8, HEAD), BF16)
    for chunk in range(CHUNKS):
        picked = slice(chunk * COLS, (chunk + 1) * COLS)
        count = NEAR_ROWS - ROWS + (chunk + 1) * CHUNK
        delta = 0.0
        for piece in split_three(
            grad_ref[picked, :].astype(F32) * forward_ref[picked, :].astype(F32)
        ):
            delta = delta + matmul_nt(ones, piece)
        score = scores[chunk, :count, :]
        top = jnp.max(score, axis=0, keepdims=True)
        weights = jnp.exp((score - top) * SCALE)
        near_p[chunk, :count, :] = weights
        stats[0:1, picked] = top
        stats[1:2, picked] = jnp.sum(weights, axis=0, keepdims=True)
        stats[2:3, picked] = delta[0:1]
        near_u[chunk, :count, :] = matmul_nt(values[:count, :], wide_g[picked, :]) - delta[0:1]


def far_kernel(
    place_ref,
    code4,
    code3,
    code2,
    code1,
    code0,
    cos_ref,
    sin_ref,
    steps_ref,
    had_ref,
    wide_q,
    wide_g,
    near_p,
    near_u,
    stats,
    near_t,
    raw_ref,
    back_out,
    parts,
    query_hbm,
    keys,
    keys_t,
    values,
    scores,
    lows,
    key_acc,
    value_acc,
    grads,
    query_out,
    sems,
):
    hadamard = had_ref[...]
    tables = (cos_ref, sin_ref)
    for block, code_ref in enumerate((code4, code3)):
        made = dequantize(code_ref, tables, block, steps_ref, hadamard)
        store_block(made, block * ROWS, keys, keys_t, values)
    edge_row = lax.broadcasted_iota(jnp.int32, (CHUNK, COLS), 0)
    edge_token = lax.broadcasted_iota(jnp.int32, (CHUNK, COLS), 1) // QUERY_HEADS
    for chunk in range(CHUNKS):
        picked = slice(chunk * COLS, (chunk + 1) * COLS)
        first = chunk * CHUNK
        score = matmul_nt(keys[first:, :], wide_q[picked, :])
        scores[chunk, first : first + CHUNK, :] = jnp.where(
            edge_row > edge_token, score[:CHUNK], FLOOR
        )
        scores[chunk, first + CHUNK :, :] = score[CHUNK:]

    missing = WIN - place_ref[0] * ROWS

    @pl.when(missing > 0)
    def _():
        row = lax.broadcasted_iota(jnp.int32, (FAR_ROWS, COLS), 0)
        for chunk in range(CHUNKS):
            scores[chunk] = jnp.where(row < missing, FLOOR, scores[chunk])

    key_acc[...] = jnp.zeros_like(key_acc)
    value_acc[...] = jnp.zeros_like(value_acc)
    grads[...] = jnp.zeros_like(grads)
    low_lane = (
        lax.broadcasted_iota(jnp.int32, (HEAD, COLS), 1) % QUERY_HEADS < QUERY_HEADS // KV_HEADS
    )
    copies = []
    for chunk in range(CHUNKS):
        picked = slice(chunk * COLS, (chunk + 1) * COLS)
        first = chunk * CHUNK
        count = NEAR_ROWS - ROWS + (chunk + 1) * CHUNK
        last = FAR_ROWS + count
        score = scores[chunk, first:, :]
        near_top = stats[0:1, picked]
        top = jnp.maximum(near_top, jnp.max(score, axis=0, keepdims=True))
        far = jnp.exp((score - top) * SCALE)
        kept = jnp.exp((near_top - top) * SCALE)
        inverse = 1.0 / (stats[1:2, picked] * kept + jnp.sum(far, axis=0, keepdims=True))
        far = far * inverse
        near = near_p[chunk, :count, :] * (kept * inverse)
        upstream = matmul_nt(values[first:, :], wide_g[picked, :]) - stats[2:3, picked]
        lows[chunk, first:FAR_ROWS, :] = far.astype(BF16)
        lows[chunk, FAR_ROWS:last, :] = near.astype(BF16)
        grads[chunk, first:FAR_ROWS, :] = (far * upstream).astype(BF16)
        grads[chunk, FAR_ROWS:last, :] = (near * near_u[chunk, :count, :]).astype(BF16)
        value_acc[first:last, :] += matmul(lows[chunk, first:last, :], wide_g[picked, :])
        key_acc[first:last, :] += matmul(grads[chunk, first:last, :], wide_q[picked, :])
        both = matmul(keys_t[...], grads[chunk, :FAR_ROWS, :])
        both = both + matmul(near_t[...], grads[chunk, FAR_ROWS:, :])
        query_grad = jnp.where(low_lane, both[:HEAD], both[HEAD:]) * SCALE
        query_out[picked, :] = query_grad.T.astype(BF16)
        rows = pl.ds(chunk * COLS, COLS)
        copies.append(
            pltpu.make_async_copy(query_out.at[rows], query_hbm.at[rows], sems.at[chunk])
        )
        copies[-1].start()

    code_refs = (code4, code3, code2, code1, code0)
    outs = [back_out.at[:ROWS], back_out.at[ROWS:]]
    outs = outs + [parts.at[block * ROWS : (block + 1) * ROWS] for block in range(3)]
    for head in range(KV_HEADS):
        cols = head_cols(head)
        value_cols = head_cols(KV_HEADS + head)
        sums = [0.0, 0.0, 0.0, 0.0]
        for block in range(BLOCKS):
            rows = slice(block * ROWS, (block + 1) * ROWS)
            out = outs[block]
            part = key_acc[rows, cols] * SCALE
            part = part * cos_ref[rows, :] - pltpu.roll(part, HEAD // 2, 1) * sin_ref[rows, :]
            out[:, cols] = part.astype(out.dtype)
            code = code_refs[block][:, cols].astype(F32)
            sums[0] = sums[0] + jnp.sum(part * code, axis=0, keepdims=True)
            sums[1] = sums[1] - jnp.sum(part, axis=0, keepdims=True)
            total = 0.0
            for piece in split_two(value_acc[rows, cols]):
                total = total + matmul(piece, hadamard)
            part = total * SCALE
            out[:, value_cols] = part.astype(out.dtype)
            code = code_refs[block][:, value_cols].astype(F32)
            sums[2] = sums[2] + jnp.sum(part * code, axis=0, keepdims=True)
            sums[3] = sums[3] - jnp.sum(part, axis=0, keepdims=True)
        for term in range(4):
            row = term * KV_HEADS + head
            for copy in range(raw_ref.shape[0]):
                raw_ref[copy, row : row + 1, :] = sums[term]
    for copy in copies:
        copy.wait()


def middle_kernel(parts, back_ref, mid_ref, near_ref):
    total = parts[: 2 * ROWS, :] + back_ref[...].astype(F32)
    mid_ref[...] = total[:ROWS].astype(BF16)
    near_ref[...] = total[ROWS:].astype(BF16)


def spread_kernel(in_ref, raw_ref):
    per_head = in_ref.shape[0] // 2
    terms = 4 * KV_HEADS
    for head in range(2):
        total = jnp.sum(in_ref[head * per_head : (head + 1) * per_head], axis=0)
        shape = (raw_ref.shape[0], terms, HEAD)
        raw_ref[:, head * terms : (head + 1) * terms, :] = jnp.broadcast_to(total[None], shape)


def clip_kernel(first_ref, all_ref, quant_out):
    total = jnp.sum(all_ref[...], axis=0)
    squares = jnp.sum(total * total, keepdims=True)
    mine = jnp.where(first_ref[...] > 0.0, total[: 4 * KV_HEADS], total[4 * KV_HEADS :])
    quant_out[...] = mine * jnp.minimum(1.0, clip_limit / jnp.sqrt(squares + 1e-06))


def add_kernel(parts, mid_ref, sum_ref):
    sum_ref[...] = parts[2 * ROWS :, :] + mid_ref[...].astype(F32)


def finish_kernel(first_ref, sum_ref, near_ref, code_ref, key_out, value_out, first_out, rows_ref):
    first_out[...] = first_ref[...]
    total = sum_ref[...] + near_ref[...].astype(F32)
    code = code_ref[...].astype(F32)
    total = jnp.where((code > 0.0) & (code < 15.0), total, 0.0)
    for kind, out in enumerate((key_out, value_out)):
        for head in range(KV_HEADS):
            rows_ref[kind, pl.ds(head, ROWS, stride=KV_HEADS), :] = total[
                :, head_cols(kind * KV_HEADS + head)
            ]
        out[...] = rows_ref[kind].astype(BF16)


def call(
    kernel, outs, scratch=(), scalars=0, inputs=(), hbm_outs=(), copies=0, limit=24, flops=None
):
    place = {"s": pltpu.SMEM, "v": pltpu.VMEM, "h": pl.ANY}
    specs = [pl.BlockSpec(memory_space=place[kind]) for kind in "s" * scalars + inputs]
    out_specs = [pl.BlockSpec(memory_space=pltpu.VMEM)] * len(outs)
    out_specs = out_specs + [pl.BlockSpec(memory_space=pltpu.HBM)] * len(hbm_outs)
    outs = list(outs) + list(hbm_outs)
    scratch_shapes = [pltpu.VMEM(shape, dtype) for shape, dtype in scratch]
    if copies:
        scratch_shapes.append(pltpu.SemaphoreType.DMA((copies,)))
    params, cost = {}, None
    if flops is not None:
        cost = pl.CostEstimate(flops=flops, bytes_accessed=0, transcendentals=0)
    if limit:
        params["vmem_limit_bytes"] = limit * 1024 * 1024
    return pl.pallas_call(
        kernel,
        out_shape=[jax.ShapeDtypeStruct(shape, dtype) for shape, dtype in outs],
        in_specs=specs,
        out_specs=out_specs,
        scratch_shapes=scratch_shapes,
        compiler_params=pltpu.CompilerParams(**params),
        cost_estimate=cost,
    )


def rope_tables(positions, head_size):
    freqs = rope_base ** (-jnp.arange(0, head_size, 2, dtype=jnp.float32) / head_size)
    angles = positions.astype(jnp.float32)[:, None] * freqs[None, :]
    cosines, sines = jnp.cos(angles), jnp.sin(angles)
    return (
        jnp.concatenate([cosines, cosines], axis=-1),
        jnp.concatenate([-sines, sines], axis=-1),
    )


def hadamard_signs(order):
    index = jnp.arange(order, dtype=jnp.int32)
    common = jnp.bitwise_and(index[:, None], index[None, :])
    parity = jnp.zeros((order, order), jnp.int32)
    for level in range(order.bit_length() - 1):
        parity = parity + jnp.bitwise_and(jnp.right_shift(common, level), 1)
    return (1 - 2 * (parity % 2)).astype(BF16)


def body(query, grad_out, out_forward, k_codes, k_scale, k_offset, v_codes, v_scale, v_offset):
    device_block = jnp.int32(0)
    for axis in TOK:
        device_block = device_block * lax.axis_size(axis) + lax.axis_index(axis)
    place = device_block.astype(jnp.int32).reshape(1)
    flat_codes = (KV_HEADS * ROWS, HEAD)
    flat_rows = (QUERY_HEADS * ROWS, HEAD)
    pack = (ROWS, 2 * WIDE)

    (own,) = call(
        pack_kernel, [(pack, BF16)], [((2,) + flat_codes, jnp.int32)], inputs="hh", copies=2 * PIECES, limit=0
    )(k_codes.reshape(flat_codes), v_codes.reshape(flat_codes))
    two = shift(own, 2)
    one = shift(own, 1)
    queries = query.reshape(flat_rows)
    upstream_rows = grad_out.reshape(flat_rows)
    first_row = device_block * ROWS - WIN
    cosines, sines = rope_tables(first_row + jnp.arange(SPAN, dtype=jnp.int32), HEAD)
    steps = jnp.stack([k_scale, k_offset, v_scale, v_offset]).reshape(4, WIDE)
    hadamard = hadamard_signs(HEAD)
    four = shift(two, 2)
    three = shift(two, 1)

    wide = (QUERY_HEADS * ROWS, WIDE)
    near_pairs = (CHUNKS, NEAR_ROWS, COLS)
    wide_q, wide_g, near_t, near_p, near_u, stats = call(
        near_kernel,
        [
            (wide, BF16),
            (wide, BF16),
            ((WIDE, NEAR_ROWS), BF16),
            (near_pairs, F32),
            (near_pairs, F32),
            ((8, QUERY_HEADS * ROWS), F32),
        ],
        scratch=[
            ((NEAR_ROWS, WIDE), BF16),
            ((NEAR_ROWS, WIDE), BF16),
            (near_pairs, F32),
        ],
        scalars=1,
        inputs="v" * 10,
    )(
        place,
        queries,
        upstream_rows,
        out_forward.reshape(flat_rows),
        two,
        one,
        own,
        cosines,
        sines,
        steps,
        hadamard,
    )
    raw, back, parts, query_grad = call(
        far_kernel,
        [
            ((axis_count(FLAT), 4 * KV_HEADS, HEAD), F32),
            ((2 * ROWS, 2 * WIDE), BF16),
            ((3 * ROWS, 2 * WIDE), F32),
        ],
        scratch=[
            ((FAR_ROWS, WIDE), BF16),
            ((WIDE, FAR_ROWS), BF16),
            ((FAR_ROWS, WIDE), BF16),
            ((CHUNKS, FAR_ROWS, COLS), F32),
            ((CHUNKS, SPAN, COLS), BF16),
            ((SPAN, WIDE), F32),
            ((SPAN, WIDE), F32),
            ((CHUNKS, SPAN, COLS), BF16),
            (flat_rows, BF16),
        ],
        scalars=1,
        inputs="v" * 15,
        hbm_outs=[(flat_rows, BF16)],
        copies=CHUNKS,
    )(
        place,
        four,
        three,
        two,
        one,
        own,
        cosines,
        sines,
        steps,
        hadamard,
        wide_q,
        wide_g,
        near_p,
        near_u,
        stats,
        near_t,
    )
    back = shift(back, -2)
    raw = lax.all_to_all(raw, FLAT, 0, 0)
    columns = axis_count(("z",))
    (raw,) = call(spread_kernel, [((columns, 8 * KV_HEADS, HEAD), F32)], inputs="v")(raw)
    mid, near = call(middle_kernel, [(pack, BF16)] * 2, inputs="vv", flops=MIDDLE_FLOPS)(parts, back)
    mid = shift(mid, -2)
    near = shift(near, -1)
    raw = lax.all_to_all(raw, "z", 0, 0)
    first = jnp.where(lax.axis_index("head") == 0, jnp.ones((4 * KV_HEADS, HEAD), F32), 0.0)
    (own_sum,) = call(add_kernel, [(pack, F32)], inputs="vv", flops=ADD_FLOPS)(parts, mid)
    key_grad, value_grad, first = call(
        finish_kernel,
        [(flat_codes, BF16)] * 2 + [((4 * KV_HEADS, HEAD), F32)],
        scratch=[((2,) + flat_codes, F32)],
        inputs="vvvv",
        flops=FINISH_FLOPS,
    )(first, own_sum, near, own)
    (quant,) = call(clip_kernel, [((4 * KV_HEADS, HEAD), F32)], inputs="vv")(first, raw)
    return (
        query_grad.reshape(ROWS, QUERY_HEADS, HEAD),
        key_grad.reshape(ROWS, KV_HEADS, HEAD),
        value_grad.reshape(ROWS, KV_HEADS, HEAD),
        quant.reshape(4, KV_HEADS, HEAD),
    )


def solution(mesh):
    sizes = (mesh.shape["head"], mesh.shape["outer"] // 2, 2, 2, mesh.shape["inner"] // 2)
    split = Mesh(mesh.devices.reshape(sizes), ("head",) + TOK)
    rows = P(TOK, "head", None)
    steps = P("head", None)
    return jax.shard_map(
        body,
        mesh=split,
        in_specs=(rows, rows, rows, rows, steps, steps, rows, steps, steps),
        out_specs=(rows, rows, rows, P(None, "head", None)),
        check_vma=False,
    )
```

```python
import math

import jax
import jax.numpy as jnp
from jax import lax
from jax.experimental import pallas as pl
from jax.experimental.pallas import tpu as pltpu
from jax.sharding import Mesh, PartitionSpec as P

WIN = 512
ROWS = 128
HEAD = 128
QUERY_HEADS = 16
KV_HEADS = 2
BLOCKS = WIN // ROWS + 1
SPAN = BLOCKS * ROWS
WIDE = KV_HEADS * HEAD
CHUNK = 32
COLS = CHUNK * QUERY_HEADS
CHUNKS = ROWS // CHUNK
FAR_BLOCKS = 2
PIECES = 4
PACK_LIMIT = 0
FINISH_FLOPS = None
ADD_FLOPS = None
MIDDLE_FLOPS = 2 * 10**9
FAR_ROWS = FAR_BLOCKS * ROWS
NEAR_ROWS = SPAN - FAR_ROWS
SCALE = 1.0 / math.sqrt(HEAD)
FLOOR = -3.0e38
clip_limit = 16.0
rope_base = 500000.0
TOK = ("x", "core", "ylo", "z")
FLAT = ("head", "x", "core", "ylo")
F32 = jnp.float32
BF16 = jnp.bfloat16


def shift(value, by):
    count = 1
    for axis in TOK:
        count *= lax.axis_size(axis)
    pairs = [(i, i + by) for i in range(count) if 0 <= i + by < count]
    return lax.ppermute(value, TOK, pairs)


def axis_count(axes):
    count = 1
    for axis in axes:
        count *= lax.axis_size(axis)
    return count


def split_two(value):
    high = value.astype(BF16)
    return high, (value - high.astype(F32)).astype(BF16)


def split_three(value):
    high = value.astype(BF16)
    rest = value - high.astype(F32)
    middle = rest.astype(BF16)
    return high, middle, (rest - middle.astype(F32)).astype(BF16)


def matmul(left, right):
    return jnp.dot(left, right, preferred_element_type=F32)


def matmul_nt(left, right):
    return lax.dot_general(left, right, (((1,), (1,)), ((), ())), preferred_element_type=F32)


def head_cols(head):
    return slice(head * HEAD, (head + 1) * HEAD)


def pack_kernel(key_hbm, value_hbm, out_ref, rows_ref, sems):
    copies = []
    step = KV_HEADS * ROWS // PIECES
    for kind, source in enumerate((key_hbm, value_hbm)):
        for piece in range(PIECES):
            rows = pl.ds(piece * step, step)
            copies.append(
                pltpu.make_async_copy(
                    source.at[rows], rows_ref.at[kind, rows], sems.at[kind * PIECES + piece]
                )
            )
            copies[-1].start()
    for kind in range(2):
        for piece in range(PIECES):
            copies[kind * PIECES + piece].wait()
        for head in range(KV_HEADS):
            code = rows_ref[kind, pl.ds(head, ROWS, stride=KV_HEADS), :].astype(F32)
            out_ref[:, head_cols(kind * KV_HEADS + head)] = code.astype(BF16)


def widen(rows, low):
    zero = jnp.zeros_like(rows)
    return jnp.concatenate([jnp.where(low, rows, zero), jnp.where(low, zero, rows)], axis=1)


def dequantize(code_ref, tables, block, steps_ref, hadamard):
    rows = slice(block * ROWS, (block + 1) * ROWS)
    cos_ref, sin_ref = tables
    cosines, sines = cos_ref[rows, :], sin_ref[rows, :]
    keys, values = [], []
    for head in range(KV_HEADS):
        cols = head_cols(head)
        code = code_ref[:, cols].astype(F32)
        deq = steps_ref[0:1, cols] * code - steps_ref[1:2, cols]
        keys.append(deq * cosines + pltpu.roll(deq, HEAD // 2, 1) * sines)
        code = code_ref[:, head_cols(KV_HEADS + head)].astype(F32)
        deq = steps_ref[2:3, cols] * code - steps_ref[3:4, cols]
        total = 0.0
        for piece in split_three(deq):
            total = total + matmul(piece, hadamard)
        values.append((total * SCALE).astype(BF16))
    return keys, values


def store_block(dequantized, row, keys, keys_t, values):
    rows = slice(row, row + ROWS)
    for head in range(KV_HEADS):
        cols = head_cols(head)
        keys[rows, cols] = dequantized[0][head].astype(BF16)
        keys_t[cols, rows] = dequantized[0][head].T.astype(BF16)
        values[rows, cols] = dequantized[1][head]


def near_kernel(
    place_ref,
    query_ref,
    grad_ref,
    forward_ref,
    code2,
    code1,
    code0,
    cos_ref,
    sin_ref,
    steps_ref,
    had_ref,
    wide_q,
    wide_g,
    keys_t,
    near_p,
    near_u,
    stats,
    keys,
    values,
    scores,
):
    hadamard = had_ref[...]
    tables = (cos_ref, sin_ref)
    for block, code_ref in enumerate((code2, code1, code0)):
        made = dequantize(code_ref, tables, FAR_BLOCKS + block, steps_ref, hadamard)
        store_block(made, block * ROWS, keys, keys_t, values)
    low = lax.broadcasted_iota(jnp.int32, (COLS, HEAD), 0) % QUERY_HEADS < QUERY_HEADS // KV_HEADS
    edge_row = lax.broadcasted_iota(jnp.int32, (CHUNK, COLS), 0)
    edge_token = lax.broadcasted_iota(jnp.int32, (CHUNK, COLS), 1) // QUERY_HEADS
    for chunk in range(CHUNKS):
        picked = slice(chunk * COLS, (chunk + 1) * COLS)
        count = NEAR_ROWS - ROWS + (chunk + 1) * CHUNK
        wide_q[picked, :] = widen(query_ref[picked, :], low)
        wide_g[picked, :] = widen(grad_ref[picked, :], low)
        score = matmul_nt(keys[:count, :], wide_q[picked, :])
        last = count - CHUNK
        scores[chunk, :last, :] = score[:last]
        scores[chunk, last:count, :] = jnp.where(edge_row <= edge_token, score[last:], FLOOR)

    missing = (BLOCKS - FAR_BLOCKS - 1 - place_ref[0]) * ROWS

    @pl.when(missing > 0)
    def _():
        row = lax.broadcasted_iota(jnp.int32, (NEAR_ROWS, COLS), 0)
        for chunk in range(CHUNKS):
            scores[chunk] = jnp.where(row < missing, FLOOR, scores[chunk])

    ones = jnp.ones((8, HEAD), BF16)
    for chunk in range(CHUNKS):
        picked = slice(chunk * COLS, (chunk + 1) * COLS)
        count = NEAR_ROWS - ROWS + (chunk + 1) * CHUNK
        delta = 0.0
        for piece in split_three(
            grad_ref[picked, :].astype(F32) * forward_ref[picked, :].astype(F32)
        ):
            delta = delta + matmul_nt(ones, piece)
        score = scores[chunk, :count, :]
        top = jnp.max(score, axis=0, keepdims=True)
        weights = jnp.exp((score - top) * SCALE)
        near_p[chunk, :count, :] = weights
        stats[0:1, picked] = top
        stats[1:2, picked] = jnp.sum(weights, axis=0, keepdims=True)
        stats[2:3, picked] = delta[0:1]
        near_u[chunk, :count, :] = matmul_nt(values[:count, :], wide_g[picked, :]) - delta[0:1]


def far_kernel(
    place_ref,
    code4,
    code3,
    code2,
    code1,
    code0,
    cos_ref,
    sin_ref,
    steps_ref,
    had_ref,
    wide_q,
    wide_g,
    near_p,
    near_u,
    stats,
    near_t,
    raw_ref,
    back_out,
    parts,
    query_hbm,
    keys,
    keys_t,
    values,
    scores,
    lows,
    key_acc,
    value_acc,
    grads,
    query_out,
    sems,
):
    hadamard = had_ref[...]
    tables = (cos_ref, sin_ref)
    for block, code_ref in enumerate((code4, code3)):
        made = dequantize(code_ref, tables, block, steps_ref, hadamard)
        store_block(made, block * ROWS, keys, keys_t, values)
    edge_row = lax.broadcasted_iota(jnp.int32, (CHUNK, COLS), 0)
    edge_token = lax.broadcasted_iota(jnp.int32, (CHUNK, COLS), 1) // QUERY_HEADS
    for chunk in range(CHUNKS):
        picked = slice(chunk * COLS, (chunk + 1) * COLS)
        first = chunk * CHUNK
        score = matmul_nt(keys[first:, :], wide_q[picked, :])
        scores[chunk, first : first + CHUNK, :] = jnp.where(
            edge_row > edge_token, score[:CHUNK], FLOOR
        )
        scores[chunk, first + CHUNK :, :] = score[CHUNK:]

    missing = WIN - place_ref[0] * ROWS

    @pl.when(missing > 0)
    def _():
        row = lax.broadcasted_iota(jnp.int32, (FAR_ROWS, COLS), 0)
        for chunk in range(CHUNKS):
            scores[chunk] = jnp.where(row < missing, FLOOR, scores[chunk])

    key_acc[...] = jnp.zeros_like(key_acc)
    value_acc[...] = jnp.zeros_like(value_acc)
    grads[...] = jnp.zeros_like(grads)
    low_lane = (
        lax.broadcasted_iota(jnp.int32, (HEAD, COLS), 1) % QUERY_HEADS < QUERY_HEADS // KV_HEADS
    )
    copies = []
    for chunk in range(CHUNKS):
        picked = slice(chunk * COLS, (chunk + 1) * COLS)
        first = chunk * CHUNK
        count = NEAR_ROWS - ROWS + (chunk + 1) * CHUNK
        last = FAR_ROWS + count
        score = scores[chunk, first:, :]
        near_top = stats[0:1, picked]
        top = jnp.maximum(near_top, jnp.max(score, axis=0, keepdims=True))
        far = jnp.exp((score - top) * SCALE)
        kept = jnp.exp((near_top - top) * SCALE)
        inverse = 1.0 / (stats[1:2, picked] * kept + jnp.sum(far, axis=0, keepdims=True))
        far = far * inverse
        near = near_p[chunk, :count, :] * (kept * inverse)
        upstream = matmul_nt(values[first:, :], wide_g[picked, :]) - stats[2:3, picked]
        lows[chunk, first:FAR_ROWS, :] = far.astype(BF16)
        lows[chunk, FAR_ROWS:last, :] = near.astype(BF16)
        grads[chunk, first:FAR_ROWS, :] = (far * upstream).astype(BF16)
        grads[chunk, FAR_ROWS:last, :] = (near * near_u[chunk, :count, :]).astype(BF16)
        value_acc[first:last, :] += matmul(lows[chunk, first:last, :], wide_g[picked, :])
        key_acc[first:last, :] += matmul(grads[chunk, first:last, :], wide_q[picked, :])
        both = matmul(keys_t[...], grads[chunk, :FAR_ROWS, :])
        both = both + matmul(near_t[...], grads[chunk, FAR_ROWS:, :])
        query_grad = jnp.where(low_lane, both[:HEAD], both[HEAD:]) * SCALE
        query_out[picked, :] = query_grad.T.astype(BF16)
        rows = pl.ds(chunk * COLS, COLS)
        copies.append(
            pltpu.make_async_copy(query_out.at[rows], query_hbm.at[rows], sems.at[chunk])
        )
        copies[-1].start()

    code_refs = (code4, code3, code2, code1, code0)
    outs = [back_out.at[:ROWS], back_out.at[ROWS:]]
    outs = outs + [parts.at[block * ROWS : (block + 1) * ROWS] for block in range(3)]
    for head in range(KV_HEADS):
        cols = head_cols(head)
        value_cols = head_cols(KV_HEADS + head)
        sums = [0.0, 0.0, 0.0, 0.0]
        for block in range(BLOCKS):
            rows = slice(block * ROWS, (block + 1) * ROWS)
            out = outs[block]
            part = key_acc[rows, cols] * SCALE
            part = part * cos_ref[rows, :] - pltpu.roll(part, HEAD // 2, 1) * sin_ref[rows, :]
            out[:, cols] = part.astype(out.dtype)
            code = code_refs[block][:, cols].astype(F32)
            sums[0] = sums[0] + jnp.sum(part * code, axis=0, keepdims=True)
            sums[1] = sums[1] - jnp.sum(part, axis=0, keepdims=True)
            total = 0.0
            for piece in split_two(value_acc[rows, cols]):
                total = total + matmul(piece, hadamard)
            part = total * SCALE
            out[:, value_cols] = part.astype(out.dtype)
            code = code_refs[block][:, value_cols].astype(F32)
            sums[2] = sums[2] + jnp.sum(part * code, axis=0, keepdims=True)
            sums[3] = sums[3] - jnp.sum(part, axis=0, keepdims=True)
        for term in range(4):
            row = term * KV_HEADS + head
            for copy in range(raw_ref.shape[0]):
                raw_ref[copy, row : row + 1, :] = sums[term]
    for copy in copies:
        copy.wait()


def middle_kernel(parts, back_ref, mid_ref, near_ref):
    total = parts[: 2 * ROWS, :] + back_ref[...].astype(F32)
    mid_ref[...] = total[:ROWS].astype(BF16)
    near_ref[...] = total[ROWS:].astype(BF16)


def spread_kernel(in_ref, raw_ref):
    per_head = in_ref.shape[0] // 2
    terms = 4 * KV_HEADS
    for head in range(2):
        total = jnp.sum(in_ref[head * per_head : (head + 1) * per_head], axis=0)
        shape = (raw_ref.shape[0], terms, HEAD)
        raw_ref[:, head * terms : (head + 1) * terms, :] = jnp.broadcast_to(total[None], shape)


def clip_kernel(first_ref, all_ref, quant_out, mark_out):
    mark_out[...] = first_ref[...]
    total = jnp.sum(all_ref[...], axis=0)
    squares = jnp.sum(total * total, keepdims=True)
    mine = jnp.where(first_ref[...] > 0.0, total[: 4 * KV_HEADS], total[4 * KV_HEADS :])
    quant_out[...] = mine * jnp.minimum(1.0, clip_limit / jnp.sqrt(squares + 1e-06))


def add_kernel(parts, mid_ref, sum_ref):
    sum_ref[...] = parts[2 * ROWS :, :] + mid_ref[...].astype(F32)


def finish_kernel(mark_ref, sum_ref, near_ref, code_ref, key_out, value_out, rows_ref):
    total = sum_ref[...] + near_ref[...].astype(F32)
    code = code_ref[...].astype(F32)
    total = jnp.where((code > 0.0) & (code < 15.0), total, 0.0)
    for kind, out in enumerate((key_out, value_out)):
        for head in range(KV_HEADS):
            rows_ref[kind, pl.ds(head, ROWS, stride=KV_HEADS), :] = total[
                :, head_cols(kind * KV_HEADS + head)
            ]
        out[...] = rows_ref[kind].astype(BF16)


def call(
    kernel, outs, scratch=(), scalars=0, inputs=(), hbm_outs=(), copies=0, limit=24, flops=None
):
    place = {"s": pltpu.SMEM, "v": pltpu.VMEM, "h": pl.ANY}
    specs = [pl.BlockSpec(memory_space=place[kind]) for kind in "s" * scalars + inputs]
    out_specs = [pl.BlockSpec(memory_space=pltpu.VMEM)] * len(outs)
    out_specs = out_specs + [pl.BlockSpec(memory_space=pltpu.HBM)] * len(hbm_outs)
    outs = list(outs) + list(hbm_outs)
    scratch_shapes = [pltpu.VMEM(shape, dtype) for shape, dtype in scratch]
    if copies:
        scratch_shapes.append(pltpu.SemaphoreType.DMA((copies,)))
    params, cost = {}, None
    if flops is not None:
        cost = pl.CostEstimate(flops=flops, bytes_accessed=0, transcendentals=0)
    if limit:
        params["vmem_limit_bytes"] = limit * 1024 * 1024
    return pl.pallas_call(
        kernel,
        out_shape=[jax.ShapeDtypeStruct(shape, dtype) for shape, dtype in outs],
        in_specs=specs,
        out_specs=out_specs,
        scratch_shapes=scratch_shapes,
        compiler_params=pltpu.CompilerParams(**params),
        cost_estimate=cost,
    )


def rope_tables(positions, head_size):
    freqs = rope_base ** (-jnp.arange(0, head_size, 2, dtype=jnp.float32) / head_size)
    angles = positions.astype(jnp.float32)[:, None] * freqs[None, :]
    cosines, sines = jnp.cos(angles), jnp.sin(angles)
    return (
        jnp.concatenate([cosines, cosines], axis=-1),
        jnp.concatenate([-sines, sines], axis=-1),
    )


def hadamard_signs(order):
    index = jnp.arange(order, dtype=jnp.int32)
    common = jnp.bitwise_and(index[:, None], index[None, :])
    parity = jnp.zeros((order, order), jnp.int32)
    for level in range(order.bit_length() - 1):
        parity = parity + jnp.bitwise_and(jnp.right_shift(common, level), 1)
    return (1 - 2 * (parity % 2)).astype(BF16)


def body(query, grad_out, out_forward, k_codes, k_scale, k_offset, v_codes, v_scale, v_offset):
    device_block = jnp.int32(0)
    for axis in TOK:
        device_block = device_block * lax.axis_size(axis) + lax.axis_index(axis)
    place = device_block.astype(jnp.int32).reshape(1)
    flat_codes = (KV_HEADS * ROWS, HEAD)
    flat_rows = (QUERY_HEADS * ROWS, HEAD)
    pack = (ROWS, 2 * WIDE)

    (own,) = call(
        pack_kernel, [(pack, BF16)], [((2,) + flat_codes, jnp.int32)], inputs="hh", copies=2 * PIECES, limit=0
    )(k_codes.reshape(flat_codes), v_codes.reshape(flat_codes))
    two = shift(own, 2)
    one = shift(own, 1)
    queries = query.reshape(flat_rows)
    upstream_rows = grad_out.reshape(flat_rows)
    first_row = device_block * ROWS - WIN
    cosines, sines = rope_tables(first_row + jnp.arange(SPAN, dtype=jnp.int32), HEAD)
    steps = jnp.stack([k_scale, k_offset, v_scale, v_offset]).reshape(4, WIDE)
    hadamard = hadamard_signs(HEAD)
    four = shift(two, 2)
    three = shift(two, 1)

    wide = (QUERY_HEADS * ROWS, WIDE)
    near_pairs = (CHUNKS, NEAR_ROWS, COLS)
    wide_q, wide_g, near_t, near_p, near_u, stats = call(
        near_kernel,
        [
            (wide, BF16),
            (wide, BF16),
            ((WIDE, NEAR_ROWS), BF16),
            (near_pairs, F32),
            (near_pairs, F32),
            ((8, QUERY_HEADS * ROWS), F32),
        ],
        scratch=[
            ((NEAR_ROWS, WIDE), BF16),
            ((NEAR_ROWS, WIDE), BF16),
            (near_pairs, F32),
        ],
        scalars=1,
        inputs="v" * 10,
    )(
        place,
        queries,
        upstream_rows,
        out_forward.reshape(flat_rows),
        two,
        one,
        own,
        cosines,
        sines,
        steps,
        hadamard,
    )
    raw, back, parts, query_grad = call(
        far_kernel,
        [
            ((axis_count(FLAT), 4 * KV_HEADS, HEAD), F32),
            ((2 * ROWS, 2 * WIDE), BF16),
            ((3 * ROWS, 2 * WIDE), F32),
        ],
        scratch=[
            ((FAR_ROWS, WIDE), BF16),
            ((WIDE, FAR_ROWS), BF16),
            ((FAR_ROWS, WIDE), BF16),
            ((CHUNKS, FAR_ROWS, COLS), F32),
            ((CHUNKS, SPAN, COLS), BF16),
            ((SPAN, WIDE), F32),
            ((SPAN, WIDE), F32),
            ((CHUNKS, SPAN, COLS), BF16),
            (flat_rows, BF16),
        ],
        scalars=1,
        inputs="v" * 15,
        hbm_outs=[(flat_rows, BF16)],
        copies=CHUNKS,
    )(
        place,
        four,
        three,
        two,
        one,
        own,
        cosines,
        sines,
        steps,
        hadamard,
        wide_q,
        wide_g,
        near_p,
        near_u,
        stats,
        near_t,
    )
    back = shift(back, -2)
    raw = lax.all_to_all(raw, FLAT, 0, 0)
    columns = axis_count(("z",))
    (raw,) = call(spread_kernel, [((columns, 8 * KV_HEADS, HEAD), F32)], inputs="v")(raw)
    mid, near = call(middle_kernel, [(pack, BF16)] * 2, inputs="vv", flops=MIDDLE_FLOPS)(parts, back)
    mid = shift(mid, -2)
    near = shift(near, -1)
    raw = lax.all_to_all(raw, "z", 0, 0)
    first = jnp.where(lax.axis_index("head") == 0, jnp.ones((4 * KV_HEADS, HEAD), F32), 0.0)
    quant, mark = call(clip_kernel, [((4 * KV_HEADS, HEAD), F32)] * 2, inputs="vv")(first, raw)
    (own_sum,) = call(add_kernel, [(pack, F32)], inputs="vv", flops=ADD_FLOPS)(parts, mid)
    key_grad, value_grad = call(
        finish_kernel,
        [(flat_codes, BF16)] * 2,
        scratch=[((2,) + flat_codes, F32)],
        inputs="vvvv",
        flops=FINISH_FLOPS,
    )(mark, own_sum, near, own)
    return (
        query_grad.reshape(ROWS, QUERY_HEADS, HEAD),
        key_grad.reshape(ROWS, KV_HEADS, HEAD),
        value_grad.reshape(ROWS, KV_HEADS, HEAD),
        quant.reshape(4, KV_HEADS, HEAD),
    )


def solution(mesh):
    sizes = (mesh.shape["head"], mesh.shape["outer"] // 2, 2, 2, mesh.shape["inner"] // 2)
    split = Mesh(mesh.devices.reshape(sizes), ("head",) + TOK)
    rows = P(TOK, "head", None)
    steps = P("head", None)
    return jax.shard_map(
        body,
        mesh=split,
        in_specs=(rows, rows, rows, rows, steps, steps, rows, steps, steps),
        out_specs=(rows, rows, rows, P(None, "head", None)),
        check_vma=False,
    )
```

```python
import math

import jax
import jax.numpy as jnp
from jax import lax
from jax.experimental import pallas as pl
from jax.experimental.pallas import tpu as pltpu
from jax.sharding import Mesh, PartitionSpec as P

WIN = 512
ROWS = 128
HEAD = 128
QUERY_HEADS = 16
KV_HEADS = 2
BLOCKS = WIN // ROWS + 1
SPAN = BLOCKS * ROWS
WIDE = KV_HEADS * HEAD
CHUNK = 32
COLS = CHUNK * QUERY_HEADS
CHUNKS = ROWS // CHUNK
FAR_BLOCKS = 2
PIECES = 4
PACK_LIMIT = 0
FINISH_FLOPS = None
ADD_FLOPS = None
MIDDLE_FLOPS = 2 * 10**9
FAR_ROWS = FAR_BLOCKS * ROWS
NEAR_ROWS = SPAN - FAR_ROWS
SCALE = 1.0 / math.sqrt(HEAD)
FLOOR = -3.0e38
clip_limit = 16.0
rope_base = 500000.0
TOK = ("x", "core", "ylo", "z")
FLAT = ("head", "x", "core", "ylo")
F32 = jnp.float32
BF16 = jnp.bfloat16


def shift(value, by):
    count = 1
    for axis in TOK:
        count *= lax.axis_size(axis)
    pairs = [(i, i + by) for i in range(count) if 0 <= i + by < count]
    return lax.ppermute(value, TOK, pairs)


def axis_count(axes):
    count = 1
    for axis in axes:
        count *= lax.axis_size(axis)
    return count


def split_two(value):
    high = value.astype(BF16)
    return high, (value - high.astype(F32)).astype(BF16)


def split_three(value):
    high = value.astype(BF16)
    rest = value - high.astype(F32)
    middle = rest.astype(BF16)
    return high, middle, (rest - middle.astype(F32)).astype(BF16)


def matmul(left, right):
    return jnp.dot(left, right, preferred_element_type=F32)


def matmul_nt(left, right):
    return lax.dot_general(left, right, (((1,), (1,)), ((), ())), preferred_element_type=F32)


def head_cols(head):
    return slice(head * HEAD, (head + 1) * HEAD)


def pack_kernel(key_hbm, value_hbm, out_ref, rows_ref, sems):
    copies = []
    step = KV_HEADS * ROWS // PIECES
    for kind, source in enumerate((key_hbm, value_hbm)):
        for piece in range(PIECES):
            rows = pl.ds(piece * step, step)
            copies.append(
                pltpu.make_async_copy(
                    source.at[rows], rows_ref.at[kind, rows], sems.at[kind * PIECES + piece]
                )
            )
            copies[-1].start()
    for kind in range(2):
        for piece in range(PIECES):
            copies[kind * PIECES + piece].wait()
        for head in range(KV_HEADS):
            code = rows_ref[kind, pl.ds(head, ROWS, stride=KV_HEADS), :].astype(F32)
            out_ref[:, head_cols(kind * KV_HEADS + head)] = code.astype(BF16)


def widen(rows, low):
    zero = jnp.zeros_like(rows)
    return jnp.concatenate([jnp.where(low, rows, zero), jnp.where(low, zero, rows)], axis=1)


def dequantize(code_ref, tables, block, steps_ref, hadamard):
    rows = slice(block * ROWS, (block + 1) * ROWS)
    cos_ref, sin_ref = tables
    cosines, sines = cos_ref[rows, :], sin_ref[rows, :]
    keys, values = [], []
    for head in range(KV_HEADS):
        cols = head_cols(head)
        code = code_ref[:, cols].astype(F32)
        deq = steps_ref[0:1, cols] * code - steps_ref[1:2, cols]
        keys.append(deq * cosines + pltpu.roll(deq, HEAD // 2, 1) * sines)
        code = code_ref[:, head_cols(KV_HEADS + head)].astype(F32)
        deq = steps_ref[2:3, cols] * code - steps_ref[3:4, cols]
        total = 0.0
        for piece in split_three(deq):
            total = total + matmul(piece, hadamard)
        values.append((total * SCALE).astype(BF16))
    return keys, values


def store_block(dequantized, row, keys, keys_t, values):
    rows = slice(row, row + ROWS)
    for head in range(KV_HEADS):
        cols = head_cols(head)
        keys[rows, cols] = dequantized[0][head].astype(BF16)
        keys_t[cols, rows] = dequantized[0][head].T.astype(BF16)
        values[rows, cols] = dequantized[1][head]


def near_kernel(
    place_ref,
    query_ref,
    grad_ref,
    forward_ref,
    code2,
    code1,
    code0,
    cos_ref,
    sin_ref,
    steps_ref,
    had_ref,
    wide_q,
    wide_g,
    keys_t,
    near_p,
    near_u,
    stats,
    keys,
    values,
    scores,
):
    hadamard = had_ref[...]
    tables = (cos_ref, sin_ref)
    for block, code_ref in enumerate((code2, code1, code0)):
        made = dequantize(code_ref, tables, FAR_BLOCKS + block, steps_ref, hadamard)
        store_block(made, block * ROWS, keys, keys_t, values)
    low = lax.broadcasted_iota(jnp.int32, (COLS, HEAD), 0) % QUERY_HEADS < QUERY_HEADS // KV_HEADS
    edge_row = lax.broadcasted_iota(jnp.int32, (CHUNK, COLS), 0)
    edge_token = lax.broadcasted_iota(jnp.int32, (CHUNK, COLS), 1) // QUERY_HEADS
    for chunk in range(CHUNKS):
        picked = slice(chunk * COLS, (chunk + 1) * COLS)
        count = NEAR_ROWS - ROWS + (chunk + 1) * CHUNK
        wide_q[picked, :] = widen(query_ref[picked, :], low)
        wide_g[picked, :] = widen(grad_ref[picked, :], low)
        score = matmul_nt(keys[:count, :], wide_q[picked, :])
        last = count - CHUNK
        scores[chunk, :last, :] = score[:last]
        scores[chunk, last:count, :] = jnp.where(edge_row <= edge_token, score[last:], FLOOR)

    missing = (BLOCKS - FAR_BLOCKS - 1 - place_ref[0]) * ROWS

    @pl.when(missing > 0)
    def _():
        row = lax.broadcasted_iota(jnp.int32, (NEAR_ROWS, COLS), 0)
        for chunk in range(CHUNKS):
            scores[chunk] = jnp.where(row < missing, FLOOR, scores[chunk])

    ones = jnp.ones((8, HEAD), BF16)
    for chunk in range(CHUNKS):
        picked = slice(chunk * COLS, (chunk + 1) * COLS)
        count = NEAR_ROWS - ROWS + (chunk + 1) * CHUNK
        delta = 0.0
        for piece in split_three(
            grad_ref[picked, :].astype(F32) * forward_ref[picked, :].astype(F32)
        ):
            delta = delta + matmul_nt(ones, piece)
        score = scores[chunk, :count, :]
        top = jnp.max(score, axis=0, keepdims=True)
        weights = jnp.exp((score - top) * SCALE)
        near_p[chunk, :count, :] = weights
        stats[0:1, picked] = top
        stats[1:2, picked] = jnp.sum(weights, axis=0, keepdims=True)
        stats[2:3, picked] = delta[0:1]
        near_u[chunk, :count, :] = matmul_nt(values[:count, :], wide_g[picked, :]) - delta[0:1]


def far_kernel(
    place_ref,
    code4,
    code3,
    code2,
    code1,
    code0,
    cos_ref,
    sin_ref,
    steps_ref,
    had_ref,
    wide_q,
    wide_g,
    near_p,
    near_u,
    stats,
    near_t,
    raw_ref,
    back_out,
    parts,
    query_hbm,
    keys,
    keys_t,
    values,
    scores,
    lows,
    key_acc,
    value_acc,
    grads,
    query_out,
    sems,
):
    hadamard = had_ref[...]
    tables = (cos_ref, sin_ref)
    for block, code_ref in enumerate((code4, code3)):
        made = dequantize(code_ref, tables, block, steps_ref, hadamard)
        store_block(made, block * ROWS, keys, keys_t, values)
    edge_row = lax.broadcasted_iota(jnp.int32, (CHUNK, COLS), 0)
    edge_token = lax.broadcasted_iota(jnp.int32, (CHUNK, COLS), 1) // QUERY_HEADS
    for chunk in range(CHUNKS):
        picked = slice(chunk * COLS, (chunk + 1) * COLS)
        first = chunk * CHUNK
        score = matmul_nt(keys[first:, :], wide_q[picked, :])
        scores[chunk, first : first + CHUNK, :] = jnp.where(
            edge_row > edge_token, score[:CHUNK], FLOOR
        )
        scores[chunk, first + CHUNK :, :] = score[CHUNK:]

    missing = WIN - place_ref[0] * ROWS

    @pl.when(missing > 0)
    def _():
        row = lax.broadcasted_iota(jnp.int32, (FAR_ROWS, COLS), 0)
        for chunk in range(CHUNKS):
            scores[chunk] = jnp.where(row < missing, FLOOR, scores[chunk])

    low_lane = (
        lax.broadcasted_iota(jnp.int32, (HEAD, COLS), 1) % QUERY_HEADS < QUERY_HEADS // KV_HEADS
    )
    copies = []
    for chunk in range(CHUNKS):
        picked = slice(chunk * COLS, (chunk + 1) * COLS)
        first = chunk * CHUNK
        count = NEAR_ROWS - ROWS + (chunk + 1) * CHUNK
        last = FAR_ROWS + count
        score = scores[chunk, first:, :]
        near_top = stats[0:1, picked]
        top = jnp.maximum(near_top, jnp.max(score, axis=0, keepdims=True))
        far = jnp.exp((score - top) * SCALE)
        kept = jnp.exp((near_top - top) * SCALE)
        inverse = 1.0 / (stats[1:2, picked] * kept + jnp.sum(far, axis=0, keepdims=True))
        far = far * inverse
        near = near_p[chunk, :count, :] * (kept * inverse)
        upstream = matmul_nt(values[first:, :], wide_g[picked, :]) - stats[2:3, picked]
        lows[chunk, first:FAR_ROWS, :] = far.astype(BF16)
        lows[chunk, FAR_ROWS:last, :] = near.astype(BF16)
        grads[chunk, first:FAR_ROWS, :] = (far * upstream).astype(BF16)
        grads[chunk, FAR_ROWS:last, :] = (near * near_u[chunk, :count, :]).astype(BF16)
        if first > 0:
            grads[chunk, :first, :] = jnp.zeros((first, COLS), BF16)
        if last < SPAN:
            grads[chunk, last:, :] = jnp.zeros((SPAN - last, COLS), BF16)
        value_part = matmul(lows[chunk, first:last, :], wide_g[picked, :])
        key_part = matmul(grads[chunk, first:last, :], wide_q[picked, :])
        if chunk == 0:
            value_acc[:last, :] = value_part
            key_acc[:last, :] = key_part
            value_acc[last:, :] = jnp.zeros((SPAN - last, WIDE), F32)
            key_acc[last:, :] = jnp.zeros((SPAN - last, WIDE), F32)
        else:
            value_acc[first:last, :] += value_part
            key_acc[first:last, :] += key_part
        both = matmul(keys_t[...], grads[chunk, :FAR_ROWS, :])
        both = both + matmul(near_t[...], grads[chunk, FAR_ROWS:, :])
        query_grad = jnp.where(low_lane, both[:HEAD], both[HEAD:]) * SCALE
        query_out[picked, :] = query_grad.T.astype(BF16)
        rows = pl.ds(chunk * COLS, COLS)
        copies.append(
            pltpu.make_async_copy(query_out.at[rows], query_hbm.at[rows], sems.at[chunk])
        )
        copies[-1].start()

    code_refs = (code4, code3, code2, code1, code0)
    outs = [back_out.at[:ROWS], back_out.at[ROWS:]]
    outs = outs + [parts.at[block * ROWS : (block + 1) * ROWS] for block in range(3)]
    terms = []
    for head in range(KV_HEADS):
        cols = head_cols(head)
        value_cols = head_cols(KV_HEADS + head)
        sums = [0.0, 0.0, 0.0, 0.0]
        for block in range(BLOCKS):
            rows = slice(block * ROWS, (block + 1) * ROWS)
            out = outs[block]
            part = key_acc[rows, cols] * SCALE
            part = part * cos_ref[rows, :] - pltpu.roll(part, HEAD // 2, 1) * sin_ref[rows, :]
            out[:, cols] = part.astype(out.dtype)
            code = code_refs[block][:, cols].astype(F32)
            sums[0] = sums[0] + jnp.sum(part * code, axis=0, keepdims=True)
            sums[1] = sums[1] - jnp.sum(part, axis=0, keepdims=True)
            total = 0.0
            for piece in split_two(value_acc[rows, cols]):
                total = total + matmul(piece, hadamard)
            part = total * SCALE
            out[:, value_cols] = part.astype(out.dtype)
            code = code_refs[block][:, value_cols].astype(F32)
            sums[2] = sums[2] + jnp.sum(part * code, axis=0, keepdims=True)
            sums[3] = sums[3] - jnp.sum(part, axis=0, keepdims=True)
        terms.append(sums)
    tile = jnp.concatenate([terms[i % KV_HEADS][i // KV_HEADS] for i in range(4 * KV_HEADS)], axis=0)
    raw_ref[...] = jnp.broadcast_to(tile[None], raw_ref.shape)
    for copy in copies:
        copy.wait()


def middle_kernel(parts, back_ref, mid_ref, near_ref):
    total = parts[: 2 * ROWS, :] + back_ref[...].astype(F32)
    mid_ref[...] = total[:ROWS].astype(BF16)
    near_ref[...] = total[ROWS:].astype(BF16)


def spread_kernel(in_ref, raw_ref):
    per_head = in_ref.shape[0] // 2
    terms = 4 * KV_HEADS
    for head in range(2):
        total = jnp.sum(in_ref[head * per_head : (head + 1) * per_head], axis=0)
        shape = (raw_ref.shape[0], terms, HEAD)
        raw_ref[:, head * terms : (head + 1) * terms, :] = jnp.broadcast_to(total[None], shape)


def clip_kernel(first_ref, all_ref, quant_out, mark_out):
    mark_out[...] = first_ref[...]
    total = jnp.sum(all_ref[...], axis=0)
    squares = jnp.sum(total * total, keepdims=True)
    mine = jnp.where(first_ref[...] > 0.0, total[: 4 * KV_HEADS], total[4 * KV_HEADS :])
    quant_out[...] = mine * jnp.minimum(1.0, clip_limit / jnp.sqrt(squares + 1e-06))


def add_kernel(parts, mid_ref, sum_ref):
    sum_ref[...] = parts[2 * ROWS :, :] + mid_ref[...].astype(F32)


def finish_kernel(mark_ref, sum_ref, near_ref, code_ref, key_out, value_out, rows_ref):
    total = sum_ref[...] + near_ref[...].astype(F32)
    code = code_ref[...].astype(F32)
    total = jnp.where((code > 0.0) & (code < 15.0), total, 0.0)
    for kind, out in enumerate((key_out, value_out)):
        for head in range(KV_HEADS):
            rows_ref[kind, pl.ds(head, ROWS, stride=KV_HEADS), :] = total[
                :, head_cols(kind * KV_HEADS + head)
            ]
        out[...] = rows_ref[kind].astype(BF16)


def call(
    kernel, outs, scratch=(), scalars=0, inputs=(), hbm_outs=(), copies=0, limit=24, flops=None
):
    place = {"s": pltpu.SMEM, "v": pltpu.VMEM, "h": pl.ANY}
    specs = [pl.BlockSpec(memory_space=place[kind]) for kind in "s" * scalars + inputs]
    out_specs = [pl.BlockSpec(memory_space=pltpu.VMEM)] * len(outs)
    out_specs = out_specs + [pl.BlockSpec(memory_space=pltpu.HBM)] * len(hbm_outs)
    outs = list(outs) + list(hbm_outs)
    scratch_shapes = [pltpu.VMEM(shape, dtype) for shape, dtype in scratch]
    if copies:
        scratch_shapes.append(pltpu.SemaphoreType.DMA((copies,)))
    params, cost = {}, None
    if flops is not None:
        cost = pl.CostEstimate(flops=flops, bytes_accessed=0, transcendentals=0)
    if limit:
        params["vmem_limit_bytes"] = limit * 1024 * 1024
    return pl.pallas_call(
        kernel,
        out_shape=[jax.ShapeDtypeStruct(shape, dtype) for shape, dtype in outs],
        in_specs=specs,
        out_specs=out_specs,
        scratch_shapes=scratch_shapes,
        compiler_params=pltpu.CompilerParams(**params),
        cost_estimate=cost,
    )


def rope_tables(positions, head_size):
    freqs = rope_base ** (-jnp.arange(0, head_size, 2, dtype=jnp.float32) / head_size)
    angles = positions.astype(jnp.float32)[:, None] * freqs[None, :]
    cosines, sines = jnp.cos(angles), jnp.sin(angles)
    return (
        jnp.concatenate([cosines, cosines], axis=-1),
        jnp.concatenate([-sines, sines], axis=-1),
    )


def hadamard_signs(order):
    index = jnp.arange(order, dtype=jnp.int32)
    common = jnp.bitwise_and(index[:, None], index[None, :])
    parity = jnp.zeros((order, order), jnp.int32)
    for level in range(order.bit_length() - 1):
        parity = parity + jnp.bitwise_and(jnp.right_shift(common, level), 1)
    return (1 - 2 * (parity % 2)).astype(BF16)


def body(query, grad_out, out_forward, k_codes, k_scale, k_offset, v_codes, v_scale, v_offset):
    device_block = jnp.int32(0)
    for axis in TOK:
        device_block = device_block * lax.axis_size(axis) + lax.axis_index(axis)
    place = device_block.astype(jnp.int32).reshape(1)
    flat_codes = (KV_HEADS * ROWS, HEAD)
    flat_rows = (QUERY_HEADS * ROWS, HEAD)
    pack = (ROWS, 2 * WIDE)

    (own,) = call(
        pack_kernel, [(pack, BF16)], [((2,) + flat_codes, jnp.int32)], inputs="hh", copies=2 * PIECES, limit=0
    )(k_codes.reshape(flat_codes), v_codes.reshape(flat_codes))
    two = shift(own, 2)
    one = shift(own, 1)
    queries = query.reshape(flat_rows)
    upstream_rows = grad_out.reshape(flat_rows)
    first_row = device_block * ROWS - WIN
    cosines, sines = rope_tables(first_row + jnp.arange(SPAN, dtype=jnp.int32), HEAD)
    steps = jnp.stack([k_scale, k_offset, v_scale, v_offset]).reshape(4, WIDE)
    hadamard = hadamard_signs(HEAD)
    four = shift(two, 2)
    three = shift(two, 1)

    wide = (QUERY_HEADS * ROWS, WIDE)
    near_pairs = (CHUNKS, NEAR_ROWS, COLS)
    wide_q, wide_g, near_t, near_p, near_u, stats = call(
        near_kernel,
        [
            (wide, BF16),
            (wide, BF16),
            ((WIDE, NEAR_ROWS), BF16),
            (near_pairs, F32),
            (near_pairs, F32),
            ((8, QUERY_HEADS * ROWS), F32),
        ],
        scratch=[
            ((NEAR_ROWS, WIDE), BF16),
            ((NEAR_ROWS, WIDE), BF16),
            (near_pairs, F32),
        ],
        scalars=1,
        inputs="v" * 10,
    )(
        place,
        queries,
        upstream_rows,
        out_forward.reshape(flat_rows),
        two,
        one,
        own,
        cosines,
        sines,
        steps,
        hadamard,
    )
    raw, back, parts, query_grad = call(
        far_kernel,
        [
            ((axis_count(FLAT), 4 * KV_HEADS, HEAD), F32),
            ((2 * ROWS, 2 * WIDE), BF16),
            ((3 * ROWS, 2 * WIDE), F32),
        ],
        scratch=[
            ((FAR_ROWS, WIDE), BF16),
            ((WIDE, FAR_ROWS), BF16),
            ((FAR_ROWS, WIDE), BF16),
            ((CHUNKS, FAR_ROWS, COLS), F32),
            ((CHUNKS, SPAN, COLS), BF16),
            ((SPAN, WIDE), F32),
            ((SPAN, WIDE), F32),
            ((CHUNKS, SPAN, COLS), BF16),
            (flat_rows, BF16),
        ],
        scalars=1,
        inputs="v" * 15,
        hbm_outs=[(flat_rows, BF16)],
        copies=CHUNKS,
    )(
        place,
        four,
        three,
        two,
        one,
        own,
        cosines,
        sines,
        steps,
        hadamard,
        wide_q,
        wide_g,
        near_p,
        near_u,
        stats,
        near_t,
    )
    back = shift(back, -2)
    raw = lax.all_to_all(raw, FLAT, 0, 0)
    columns = axis_count(("z",))
    (raw,) = call(spread_kernel, [((columns, 8 * KV_HEADS, HEAD), F32)], inputs="v")(raw)
    mid, near = call(middle_kernel, [(pack, BF16)] * 2, inputs="vv", flops=MIDDLE_FLOPS)(parts, back)
    mid = shift(mid, -2)
    near = shift(near, -1)
    raw = lax.all_to_all(raw, "z", 0, 0)
    first = jnp.where(lax.axis_index("head") == 0, jnp.ones((4 * KV_HEADS, HEAD), F32), 0.0)
    quant, mark = call(clip_kernel, [((4 * KV_HEADS, HEAD), F32)] * 2, inputs="vv")(first, raw)
    (own_sum,) = call(add_kernel, [(pack, F32)], inputs="vv", flops=ADD_FLOPS)(parts, mid)
    key_grad, value_grad = call(
        finish_kernel,
        [(flat_codes, BF16)] * 2,
        scratch=[((2,) + flat_codes, F32)],
        inputs="vvvv",
        flops=FINISH_FLOPS,
    )(mark, own_sum, near, own)
    return (
        query_grad.reshape(ROWS, QUERY_HEADS, HEAD),
        key_grad.reshape(ROWS, KV_HEADS, HEAD),
        value_grad.reshape(ROWS, KV_HEADS, HEAD),
        quant.reshape(4, KV_HEADS, HEAD),
    )


def solution(mesh):
    sizes = (mesh.shape["head"], mesh.shape["outer"] // 2, 2, 2, mesh.shape["inner"] // 2)
    split = Mesh(mesh.devices.reshape(sizes), ("head",) + TOK)
    rows = P(TOK, "head", None)
    steps = P("head", None)
    return jax.shard_map(
        body,
        mesh=split,
        in_specs=(rows, rows, rows, rows, steps, steps, rows, steps, steps),
        out_specs=(rows, rows, rows, P(None, "head", None)),
        check_vma=False,
    )
```
